32 devices in a mesh: slab: 4 (over y, x), sample: 8 (over z, core).
Axes of the slice: x: 2, y: 2, z: 4, core: 2. Of those that a mesh axis runs over, the one named last changes fastest.
Arguments:
- activations: bfloat16 [8, 32, 16, 8, 128], P('sample', None, 'slab'), may hold values from -6 to 6
- grad_out: bfloat16 [8, 64, 16, 8, 128], P('sample', 'slab'), may hold values from -6 to 6
- weight: bfloat16 [27, 64, 32], replicated, may hold values from -0.21875 to 0.21875
Outputs:
- grad_inputs: bfloat16 [8, 32, 16, 8, 128], P('sample', None, 'slab')
- grad_weight: float32 [27, 64, 32], replicated
- grad_bias: float32 [64], replicated
The draws below stay inside these ranges and needn't reach their ends.
All inputs are finite; a program needn't handle non-finite values.
Results may differ from the reference program's by a relative error of at most 0.001.
Values may be sent and summed in bfloat16 or wider, within the bound.
No kernel may reach another device: no remote copies, remote signals or barrier semaphores. Data moves between devices by JAX's collectives and lax.ppermute only.
A program may use at most 64 MiB of HBM per device.

```python
import math
import jax
import jax.numpy as jnp
from jax import lax

CIN = 32
COUT = 64
NY = 8
NX = 128
SAMPLES = 8
NZ = 16


def shard_levels(own_key, shape, cuts, least, high):
    def one(dim, shards_of):
        draws = jax.random.uniform(jax.random.fold_in(jax.random.fold_in(own_key, 6), dim), (shards_of,), jnp.float32, least / len(cuts), high / len(cuts))
        return jnp.repeat(jnp.exp(draws), shape[dim] // shards_of).reshape((-1,) + (1,) * (len(shape) - dim - 1))

    gain = one(*cuts[0])
    for cut in cuts[1:]:
        gain = gain * one(*cut)
    return gain


def gaussian(stream_key, dims, scale, reach, split=(), kind=jnp.bfloat16):
    drawn = scale * jax.random.normal(stream_key, dims, jnp.float32)
    if split:
        drawn = drawn * shard_levels(stream_key, dims, split, -0.22, 0.18)
    return jnp.clip(drawn, -reach, reach).astype(kind)


def setup_inputs(seed: int = 0) -> dict:
    key_of = jax.random.split(jax.random.key(seed), 4)
    activations = gaussian(key_of[0], (SAMPLES, CIN, NZ, NY, NX), 1.0, 6.0, ((0, 8), (2, 4)))
    grad_out = gaussian(key_of[1], (SAMPLES, COUT, NZ, NY, NX), 1.0, 6.0, ((0, 8), (1, 4)))
    weight = gaussian(key_of[2], (27, COUT, CIN), (27 * CIN) ** -0.5, 0.21875)
    return dict(activations=activations, grad_out=grad_out, weight=weight)


def offsets_list():
    return [(shift_z, shift_y, shift_x) for shift_z in (-1, 0, 1) for shift_y in (-1, 0, 1) for shift_x in (-1, 0, 1)]

def one_sample(inputs, cotangent, weight):
    in_chan = inputs.shape[0]
    out_chan = cotangent.shape[0]
    planes, y_cells, x_cells = (inputs.shape[1], inputs.shape[2], inputs.shape[3])
    widths = ((0, 0), (1, 1), (1, 1), (1, 1))
    padded_in = jnp.pad(inputs, widths)
    padded_co = jnp.pad(cotangent, widths)
    center = cotangent.reshape(out_chan, -1)
    grad_in = jnp.zeros((in_chan, planes * y_cells * x_cells), jnp.float32)
    pieces = []
    for offset, (shift_z, shift_y, shift_x) in enumerate(offsets_list()):
        moved_in = padded_in[:, 1 + shift_z:1 + shift_z + planes, 1 + shift_y:1 + shift_y + y_cells, 1 + shift_x:1 + shift_x + x_cells].reshape(in_chan, -1)
        moved_co = padded_co[:, 1 - shift_z:1 - shift_z + planes, 1 - shift_y:1 - shift_y + y_cells, 1 - shift_x:1 - shift_x + x_cells].reshape(out_chan, -1)
        pieces.append(jnp.dot(center, moved_in.T, preferred_element_type=jnp.float32))
        grad_in = grad_in + jnp.dot(weight[offset].T, moved_co, preferred_element_type=jnp.float32)
    grad_in = grad_in.reshape(in_chan, planes, y_cells, x_cells).astype(jnp.bfloat16)
    return (grad_in, jnp.stack(pieces), lax.optimization_barrier(jnp.sum(center.astype(jnp.float32), axis=1)))

def reference(activations, grad_out, weight):

    def step(carry, pair):
        grad_in, wpart, bpart = one_sample(pair[0], pair[1], weight)
        return ((carry[0] + wpart, carry[1] + bpart), grad_in)
    start = (jnp.zeros((27, COUT, CIN), jnp.float32), jnp.zeros((COUT,), jnp.float32))
    totals, grad_inputs = lax.scan(step, start, (activations, grad_out))
    factor = 1.0 / math.sqrt(SAMPLES * NZ * NY * NX)
    return (grad_inputs, totals[0] * factor, totals[1] * factor)
```

```python
import functools
import math

import jax
import jax.numpy as jnp
from jax import lax
from jax.experimental import pallas as pl
from jax.experimental.pallas import tpu as pltpu
from jax.sharding import PartitionSpec as P

F32 = jnp.float32
BF16 = jnp.bfloat16
NT = (((1,), (1,)), ((), ()))


def iota(shape, dim):
    return lax.broadcasted_iota(jnp.int32, shape, dim)


def vmem():
    return pl.BlockSpec(memory_space=pltpu.VMEM)


def smem():
    return pl.BlockSpec(memory_space=pltpu.SMEM)


def filter_kernel(where, g_own, g_nbr, a_own, a_nbr, out, abuf, gbuf):
    row, col, core = where[0], where[1], where[2]
    chans = g_own.shape[0]
    r = iota((256, 256), 0)
    q = iota((256, 256), 1)
    perm_a = (((q & 7) == (r >> 5)) & ((q >> 3) == (r & 31))).astype(F32).astype(BF16)
    half = (r & 31) >> 4
    perm_g = (
        ((q & 7) == (r >> 5)) & (((q & 127) >> 3) == (r & 15)) & ((q >> 7) == jnp.where(row == 0, half, 1 - half))
    ).astype(F32).astype(BF16)
    lane = iota((256, 128), 1)

    for slot in (0, 1, 10, 11):
        abuf[slot] = jnp.zeros((96, 1024), BF16)
    for source, first in ((a_own, 2 + 4 * col), (a_nbr, 2 + 4 * (1 - col))):
        for plane in range(4):
            turned = jnp.dot(perm_a, source[:, plane].reshape(256, 128), preferred_element_type=F32).astype(BF16)
            for shift in range(3):
                for y in range(8):
                    act_y = y + shift - 1
                    piece = jnp.zeros((32, 128), BF16)
                    if 0 <= act_y < 8:
                        piece = turned[32 * act_y : 32 * act_y + 32]
                    abuf[first + plane, 32 * shift : 32 * shift + 32, 128 * y : 128 * y + 128] = piece

    gbuf[9 * row] = jnp.zeros((96, 1024), BF16)
    total = jnp.zeros((32, 128), F32)
    for plane in range(9):
        both = jnp.concatenate(
            [g_own[:, 7 * row + plane].reshape(8 * chans, 128), g_nbr[:, plane].reshape(8 * chans, 128)], axis=0
        )
        turned = jnp.dot(perm_g, both, preferred_element_type=F32)
        moved = (
            jnp.where(lane == 127, 0.0, pltpu.roll(turned, 127, 1)),
            turned,
            jnp.where(lane == 0, 0.0, pltpu.roll(turned, 1, 1)),
        )
        for shift in range(3):
            packed = moved[shift].astype(BF16)
            for y in range(8):
                gbuf[plane + 1 - row, 32 * shift : 32 * shift + 32, 128 * y : 128 * y + 128] = packed[
                    32 * y : 32 * y + 32
                ]
        cells = turned[0:32]
        for y in range(1, 8):
            cells = cells + turned[32 * y : 32 * y + 32]
        if plane == 0:
            cells = jnp.where(row == 0, cells, 0.0)
        if plane == 8:
            cells = jnp.where(row == 0, 0.0, cells)
        total = total + cells

    acc = jnp.zeros((96, 288), F32)
    for slot in range(10):
        acc = acc + lax.dot_general(
            gbuf[slot], abuf[slot : slot + 3].reshape(288, 1024), NT, preferred_element_type=F32
        )

    tail = jnp.concatenate([acc[24 * m : 24 * m + 24, 256:288] for m in range(4)], axis=1)
    column = jnp.sum(total, axis=1, keepdims=True)
    line = jnp.sum(jnp.where(iota((32, 128), 0) == iota((32, 128), 1), column, 0.0), axis=0, keepdims=True)
    bias = jnp.where(iota((8, 128), 0) == 0, line, 0.0)
    out[core] = jnp.concatenate([acc[:, 0:128], acc[0:16, 128:256]], axis=0)
    out[1 - core] = jnp.concatenate([acc[16:96, 128:256], tail, bias], axis=0)


def filter_partial(where, g_own, g_nbr, a_own, a_nbr):
    return pl.pallas_call(
        filter_kernel,
        out_shape=jax.ShapeDtypeStruct((2, 112, 128), F32),
        in_specs=[smem()] + [vmem()] * 4,
        out_specs=vmem(),
        scratch_shapes=[pltpu.VMEM((12, 96, 1024), BF16), pltpu.VMEM((10, 96, 1024), BF16)],
        compiler_params=pltpu.CompilerParams(vmem_limit_bytes=24 * 2**20),
        cost_estimate=pl.CostEstimate(flops=2 * 10 * 288 * 96 * 1024, bytes_accessed=2**21, transcendentals=0),
        name="filter_partial",
    )(where, g_own, g_nbr, a_own, a_nbr)


def finish_kernel(factor, where, mine, other, weight_out, bias_out):
    col, core = where[1], where[2]
    lane = iota((1, 128), 1)
    line = jnp.zeros((1, 128), F32)
    for x in range(2):
        which = jnp.where(col == x, 0, 1)
        a = mine[which]
        b = other[which]
        low = jnp.where(core == 0, a, b) * factor
        high = jnp.where(core == 0, b, a) * factor
        table = jnp.concatenate([low, high], axis=0)
        for nine in range(9):
            for dx in range(3):
                k = 9 * (nine // 3) + 3 * (nine % 3) + dx
                if nine < 8:
                    first = 96 * (nine // 4) + 32 * dx
                    block = table[first : first + 32, 32 * (nine % 4) : 32 * (nine % 4) + 32]
                else:
                    parts = []
                    for eight in range(4 * dx, 4 * dx + 4):
                        m, at = eight // 3, 192 + 8 * (eight % 3)
                        parts.append(table[at : at + 8, 32 * m : 32 * m + 32])
                    block = jnp.concatenate(parts, axis=0)
                weight_out[k, 16 * x : 16 * x + 16] = block[0:16]
                weight_out[k, 32 + 16 * x : 48 + 16 * x] = block[16:32]
        values = table[216:217]
        first = pltpu.roll(values, 16 * x, 1) if x else values
        second = pltpu.roll(values, 16 + 16 * x, 1)
        line = jnp.where((lane >= 16 * x) & (lane < 16 * x + 16), first, line)
        line = jnp.where((lane >= 32 + 16 * x) & (lane < 48 + 16 * x), second, line)
    bias_out[...] = line[:, 0:64]


def finish(where, mine, other, factor):
    return pl.pallas_call(
        functools.partial(finish_kernel, factor),
        out_shape=(jax.ShapeDtypeStruct((27, 64, 32), F32), jax.ShapeDtypeStruct((1, 64), F32)),
        in_specs=[smem(), vmem(), vmem()],
        out_specs=(vmem(), vmem()),
        cost_estimate=pl.CostEstimate(flops=2**18, bytes_accessed=2**20, transcendentals=0),
        name="filter_finish",
    )(where, mine, other)


def spread_kernel(where, weight, out):
    place = 2 * where[0] + where[1]
    widen = ((iota((256, 32), 0) >> 3) == iota((256, 32), 1)).astype(F32).astype(BF16)
    column = iota((64, 512), 1)
    block = column >> 7
    partner = jnp.where(block == 0, 0, jnp.where(block == 1, 2, jnp.where(block == 2, 1, 3)))
    slab = jnp.bitwise_xor(partner, place)
    repeat = (iota((64, 512), 0) == 16 * slab + ((column & 127) >> 3)).astype(F32).astype(BF16)
    gap = (iota((256, 512), 0) & 7) - (iota((256, 512), 1) & 7)
    for dz in range(3):
        for dx in range(3):
            band = jnp.zeros((256, 512), F32)
            for dy in range(3):
                tall = lax.dot_general(widen, weight[9 * dz + 3 * dy + dx], NT, preferred_element_type=F32)
                wide = jnp.dot(tall.astype(BF16), repeat, preferred_element_type=F32)
                band = jnp.where(gap == dy - 1, wide, band)
            out[3 * dz + dx] = band.astype(BF16)


def spread_filters(where, weight):
    return pl.pallas_call(
        spread_kernel,
        out_shape=jax.ShapeDtypeStruct((9, 256, 512), BF16),
        in_specs=[smem(), vmem()],
        out_specs=vmem(),
        compiler_params=pltpu.CompilerParams(vmem_limit_bytes=16 * 2**20),
        cost_estimate=pl.CostEstimate(flops=2 * 27 * 256 * 64 * 512, bytes_accessed=2**21, transcendentals=0),
        name="spread_filters",
    )(where, weight)


def input_kernel(where, spread, g_own, g_nbr, g_far, out):
    row, col = where[0], where[1]
    offset = row + col
    lane = iota((256, 128), 1)

    def plane_of(index):
        at = offset + index
        inside = (at >= 0) & (at < 6)
        at = jnp.clip(at, 0, 5)
        parts = [
            g_own[:, 7 * row + 3 * col + at].reshape(128, 128),
            g_nbr[:, 3 * col + at].reshape(128, 128),
            g_far[:, at].reshape(256, 128),
        ]
        value = jnp.concatenate(parts, axis=0)
        if index in (-1, 4):
            value = jnp.where(inside, value, jnp.zeros_like(value))
        return value

    planes = [plane_of(index) for index in range(-1, 5)]
    stacks = [jnp.concatenate([planes[1 + z - dz] for z in range(4)], axis=1) for dz in (-1, 0, 1)]
    sums = []
    for dx in range(3):
        acc = jnp.dot(spread[dx], stacks[0], preferred_element_type=F32)
        for dz in (1, 2):
            acc = acc + jnp.dot(spread[3 * dz + dx], stacks[dz], preferred_element_type=F32)
        sums.append(acc)
    for z in range(4):
        cut = slice(128 * z, 128 * z + 128)
        value = sums[1][:, cut]
        value = value + jnp.where(lane == 127, 0.0, pltpu.roll(sums[0][:, cut], 127, 1))
        value = value + jnp.where(lane == 0, 0.0, pltpu.roll(sums[2][:, cut], 1, 1))
        out[:, z] = value.astype(BF16).reshape(32, 8, 128)


def input_gradient(where, spread, g_own, g_nbr, g_far):
    return pl.pallas_call(
        input_kernel,
        out_shape=jax.ShapeDtypeStruct((32, 4, 8, 128), BF16),
        in_specs=[smem()] + [vmem()] * 4,
        out_specs=vmem(),
        compiler_params=pltpu.CompilerParams(vmem_limit_bytes=24 * 2**20),
        cost_estimate=pl.CostEstimate(flops=2 * 9 * 256 * 512 * 512, bytes_accessed=2**22, transcendentals=0),
        name="input_gradient",
    )(where, spread, g_own, g_nbr, g_far)


def swap(block, axis, bits):
    count = lax.axis_size(axis)
    return lax.ppermute(block, axis, [(i, i ^ bits) for i in range(count)])


def local_grid(activations, grad_out, weight):
    slab = lax.axis_index("slab")
    row, col = slab // 2, slab % 2
    core = lax.axis_index("sample") % 2
    where = jnp.stack([row, col, core]).astype(jnp.int32)
    act = activations[0]
    g_own = grad_out[0]

    g_out = lax.dynamic_slice_in_dim(g_own, 7 * (1 - row), 9, axis=1)
    g_nbr = swap(g_out, "slab", 2)
    a_nbr = swap(act, "slab", 1)
    spread = spread_filters(where, weight)

    g_pass = jnp.concatenate(
        [
            lax.dynamic_slice_in_dim(g_own, 7 * row + 3 * (1 - col), 6, axis=1),
            lax.dynamic_slice_in_dim(g_nbr, 3 * (1 - col), 6, axis=1),
        ],
        axis=0,
    )
    g_far = swap(g_pass, "slab", 1)

    halves = filter_partial(where, g_own, g_nbr, act, a_nbr)
    chip = halves[0] + swap(halves[1], "sample", 1)
    line = (chip + swap(chip, "sample", 2)) + (swap(chip, "sample", 4) + swap(chip, "sample", 6))
    mine = jnp.stack([line + swap(line, "slab", 2), swap(line, "slab", 1) + swap(line, "slab", 3)])
    other = swap(mine, "sample", 1)

    grad_in = input_gradient(where, spread, g_own, g_nbr, g_far)
    cells = 8 * 128 * 4 * lax.axis_size("slab") * lax.axis_size("sample")
    grad_weight, grad_bias = finish(where, mine, other, 1.0 / math.sqrt(cells))
    return grad_in[None], grad_weight, grad_bias.reshape(64)


def with_halo(block, sides, width):
    for axis, dim in sides:
        count = lax.axis_size(axis)
        forward = [(i, i + 1) for i in range(count - 1)]
        backward = [(target, source) for source, target in forward]
        low = lax.ppermute(
            lax.slice_in_dim(block, block.shape[dim] - width, None, axis=dim), axis, forward
        )
        high = lax.ppermute(lax.slice_in_dim(block, 0, width, axis=dim), axis, backward)
        block = jnp.concatenate([low, block, high], axis=dim)
    return block


def offsets_list():
    return [
        (shift_z, shift_y, shift_x)
        for shift_z in (-1, 0, 1)
        for shift_y in (-1, 0, 1)
        for shift_x in (-1, 0, 1)
    ]


def local_any(activations, grad_out, weight):
    samples, in_chan, planes, y_cells, x_cells = activations.shape
    slabs = lax.axis_size("slab")
    regrouped = lax.all_to_all(grad_out, "slab", split_axis=2, concat_axis=1, tiled=True)
    g_ext = with_halo(regrouped, (("slab", 2),), 1)
    widths = ((0, 0), (0, 0), (0, 0), (1, 1), (1, 1))
    padded_co = jnp.pad(g_ext, widths)
    grad_in = jnp.zeros((samples, in_chan, planes, y_cells, x_cells), F32)
    pieces = []
    for offset, (shift_z, shift_y, shift_x) in enumerate(offsets_list()):
        moved_co = padded_co[
            :,
            :,
            1 - shift_z : 1 - shift_z + planes,
            1 - shift_y : 1 - shift_y + y_cells,
            1 - shift_x : 1 - shift_x + x_cells,
        ]
        pieces.append(jnp.einsum("sozyx,sizyx->oi", moved_co, activations, preferred_element_type=F32))
        grad_in = grad_in + jnp.einsum("oi,sozyx->sizyx", weight[offset], moved_co, preferred_element_type=F32)
    wpart = jnp.stack(pieces)
    bpart = jnp.sum(regrouped.astype(F32), axis=(0, 2, 3, 4))
    wtotal, btotal = lax.psum((wpart, bpart), ("slab", "sample"))
    all_cells = samples * lax.axis_size("sample") * planes * slabs * y_cells * x_cells
    factor = 1.0 / math.sqrt(all_cells)
    return (grad_in.astype(BF16), wtotal * factor, btotal * factor)


def local(activations, grad_out, weight):
    grid = (
        lax.axis_size("slab") == 4
        and lax.axis_size("sample") == 8
        and activations.shape == (1, 32, 4, 8, 128)
        and grad_out.shape == (1, 16, 16, 8, 128)
    )
    return (local_grid if grid else local_any)(activations, grad_out, weight)


def solution(mesh):
    placed = (P("sample", None, "slab", None, None), P("sample", "slab", None, None, None), P())
    return jax.shard_map(
        local,
        mesh=mesh,
        in_specs=placed,
        out_specs=(P("sample", None, "slab", None, None), P(), P()),
        check_vma=False,
    )
```

```python
import functools
import math

import jax
import jax.numpy as jnp
from jax import lax
from jax.experimental import pallas as pl
from jax.experimental.pallas import tpu as pltpu
from jax.sharding import PartitionSpec as P

F32 = jnp.float32
BF16 = jnp.bfloat16
NT = (((1,), (1,)), ((), ()))


def iota(shape, dim):
    return lax.broadcasted_iota(jnp.int32, shape, dim)


def vmem():
    return pl.BlockSpec(memory_space=pltpu.VMEM)


def smem():
    return pl.BlockSpec(memory_space=pltpu.SMEM)


def one(mask):
    return mask.astype(F32).astype(BF16)


def act_rows(source, put):
    r, q = iota((256, 256), 0), iota((256, 256), 1)
    perm = one(((q & 7) == (r >> 5)) & ((q >> 3) == (r & 31)))
    both = jnp.concatenate([source[:, plane].reshape(256, 128) for plane in range(4)], axis=1)
    turned = jnp.dot(perm, both, preferred_element_type=F32).astype(BF16)
    for plane in range(4):
        for shift in range(3):
            for y in range(8):
                act_y = y + shift - 1
                piece = jnp.zeros((32, 128), BF16)
                if 0 <= act_y < 8:
                    piece = turned[32 * act_y : 32 * act_y + 32, 128 * plane : 128 * plane + 128]
                put(plane, slice(32 * shift, 32 * shift + 32), slice(128 * y, 128 * y + 128), piece)


def cot_rows(source, first, row, put):
    r, q = iota((128, 128), 0), iota((128, 128), 1)
    perm = one(((q & 7) == (r >> 4)) & ((q >> 3) == (r & 15)))
    lane = iota((128, 128), 1)
    total = jnp.zeros((16, 128), F32)
    for plane in range(9):
        turned = jnp.dot(perm, source[:, first + plane].reshape(128, 128), preferred_element_type=F32)
        moved = (
            jnp.where(lane == 127, 0.0, pltpu.roll(turned, 127, 1)),
            turned,
            jnp.where(lane == 0, 0.0, pltpu.roll(turned, 1, 1)),
        )
        for shift in range(3):
            packed = moved[shift].astype(BF16)
            for y in range(8):
                put(plane, slice(16 * shift, 16 * shift + 16), slice(128 * y, 128 * y + 128), packed[16 * y : 16 * y + 16])
        cells = turned[0:16]
        for y in range(1, 8):
            cells = cells + turned[16 * y : 16 * y + 16]
        if plane == 0:
            cells = jnp.where(row == 0, cells, 0.0)
        if plane == 8:
            cells = jnp.where(row == 0, 0.0, cells)
        total = total + cells
    return total


def near_kernel(where, g_own, a_own, a_rows, g_rows, sums):
    row = where[0]
    def put_a(plane, rows, lanes, piece):
        a_rows[plane, rows, lanes] = piece
    def put_g(plane, rows, lanes, piece):
        g_rows[plane, rows, lanes] = piece
    act_rows(a_own, put_a)
    sums[...] = cot_rows(g_own, 7 * row, row, put_g)


def near_rows(where, g_own, a_own):
    return pl.pallas_call(
        near_kernel,
        out_shape=(jax.ShapeDtypeStruct((4, 96, 1024), BF16), jax.ShapeDtypeStruct((9, 48, 1024), BF16), jax.ShapeDtypeStruct((16, 128), F32)),
        in_specs=[smem(), vmem(), vmem()],
        out_specs=(vmem(), vmem(), vmem()),
        compiler_params=pltpu.CompilerParams(vmem_limit_bytes=8 * 2**20),
        cost_estimate=pl.CostEstimate(flops=2**28, bytes_accessed=2**21, transcendentals=0),
        name="near_rows",
    )(where, g_own, a_own)


def filter_kernel(where, a_rows, g_rows, sums, g_own, g_nbr, a_nbr, after, keep, send, g_pass, abuf, gbuf):
    row, col, core = where[0], where[1], where[2]
    for slot in (0, 1, 10, 11):
        abuf[slot] = jnp.zeros((96, 1024), BF16)
    gbuf[9 * row] = jnp.zeros((96, 1024), BF16)
    near, far = 2 + 4 * col, 6 - 4 * col

    def place(shift, whose):
        return pl.ds(pl.multiple_of(32 * shift + 16 * whose, 16), 16)

    for plane in range(4):
        abuf[near + plane] = a_rows[plane]
    for plane in range(9):
        for shift in range(3):
            gbuf[plane + 1 - row, place(shift, row)] = g_rows[plane, 16 * shift : 16 * shift + 16]

    def put_a(plane, rows, lanes, piece):
        abuf[far + plane, rows, lanes] = piece

    def put_g(plane, rows, lanes, piece):
        gbuf[plane + 1 - row, place(rows.start // 16, 1 - row), lanes] = piece

    act_rows(a_nbr, put_a)
    far_sums = cot_rows(g_nbr, 0, row, put_g)

    wide = jnp.zeros((192, 384), F32)
    for slot in range(0, 10, 2):
        wide = wide + lax.dot_general(
            gbuf[slot : slot + 2].reshape(192, 1024),
            abuf[slot : slot + 4].reshape(384, 1024),
            NT,
            preferred_element_type=F32,
        )
    acc = (wide[0:96, 0:288] + wide[96:192, 96:384]).T
    side = jnp.concatenate([acc[216:288, 32 * m : 32 * m + 32] for m in range(3)], axis=0)
    table = jnp.concatenate([acc[0:216], side], axis=1)
    first = jnp.where(row == 0, sums[...], far_sums)
    second = jnp.where(row == 0, far_sums, sums[...])
    column = jnp.sum(jnp.concatenate([first, second], axis=0), axis=1, keepdims=True)
    line = jnp.sum(jnp.where(iota((32, 128), 0) == iota((32, 128), 1), column, 0.0), axis=0, keepdims=True)
    bias = jnp.where(iota((8, 128), 0) == 0, line, 0.0)
    low = table[0:112]
    high = jnp.concatenate([table[112:216], bias], axis=0)
    keep[...] = jnp.where(core == 0, low, high)
    send[...] = jnp.where(core == 0, high, low)
    for plane in range(6):
        g_pass[0:16, plane] = g_own[:, 7 * row + 3 * (1 - col) + plane]
        g_pass[16:32, plane] = g_nbr[:, 3 * (1 - col) + plane]


def filter_partial(where, a_rows, g_rows, sums, g_own, g_nbr, a_nbr, after):
    return pl.pallas_call(
        filter_kernel,
        out_shape=(jax.ShapeDtypeStruct((112, 128), F32), jax.ShapeDtypeStruct((112, 128), F32), jax.ShapeDtypeStruct((32, 6, 8, 128), BF16)),
        in_specs=[smem()] + [vmem()] * 6 + [pl.BlockSpec(memory_space=pl.ANY)],
        out_specs=(vmem(), vmem(), vmem()),
        scratch_shapes=[pltpu.VMEM((12, 96, 1024), BF16), pltpu.VMEM((10, 96, 1024), BF16)],
        compiler_params=pltpu.CompilerParams(vmem_limit_bytes=14 * 2**20),
        cost_estimate=pl.CostEstimate(flops=2 * 10 * 288 * 96 * 1024, bytes_accessed=2**21, transcendentals=0),
        name="filter_partial",
    )(where, a_rows, g_rows, sums, g_own, g_nbr, a_nbr, after)


def finish_kernel(factor, where, mine, other, weight_out, bias_out):
    col, core = where[1], where[2]
    lane = iota((224, 128), 1)
    tables = []
    for x in range(2):
        which = jnp.where(col == x, 0, 1)
        a, b = mine[which], other[which]
        low, high = jnp.where(core == 0, a, b), jnp.where(core == 0, b, a)
        tables.append(jnp.concatenate([low, high], axis=0) * factor)
    even = (lane & 16) == 0
    first = jnp.where(even, tables[0], pltpu.roll(tables[1], 16, 1))
    second = jnp.where(even, pltpu.roll(tables[0], 112, 1), tables[1])
    whole = []
    for dx in range(4):
        left = pltpu.roll(first, 128 - 32 * dx, 1) if dx else first
        right = pltpu.roll(second, (160 - 32 * dx) % 128, 1) if dx != 1 else second
        whole.append(jnp.where(lane < 32, left, right))
    for nine in range(9):
        for dx in range(3):
            k = 9 * (nine // 3) + 3 * (nine % 3) + dx
            if nine < 6:
                weight_out[k] = whole[dx][32 * nine : 32 * nine + 32, 0:64]
            elif nine == 6:
                weight_out[k, 0:24] = whole[dx][192:216, 0:64]
                weight_out[k, 24:32] = whole[3][72 * dx : 72 * dx + 8, 0:64]
            else:
                at = 72 * dx + 32 * nine - 216
                weight_out[k] = whole[3][at : at + 32, 0:64]
    bias_out[...] = whole[0][216:217, 0:64]


def finish(where, mine, other, factor):
    return pl.pallas_call(
        functools.partial(finish_kernel, factor),
        out_shape=(jax.ShapeDtypeStruct((27, 32, 64), F32), jax.ShapeDtypeStruct((1, 64), F32)),
        in_specs=[smem(), vmem(), vmem()],
        out_specs=(vmem(), vmem()),
        compiler_params=pltpu.CompilerParams(vmem_limit_bytes=4 * 2**20),
        cost_estimate=pl.CostEstimate(flops=2**18, bytes_accessed=2**20, transcendentals=0),
        name="filter_finish",
    )(where, mine, other)


def spread_kernel(where, weight, out):
    place = 2 * where[0] + where[1]
    column = iota((64, 512), 1)
    block = column >> 7
    partner = jnp.where(block == 0, 0, jnp.where(block == 1, 2, jnp.where(block == 2, 1, 3)))
    slab = jnp.bitwise_xor(partner, place)
    repeat = one(iota((64, 512), 0) == 16 * slab + ((column & 127) >> 3))
    gap = iota((8, 128), 0) - (iota((8, 128), 1) & 7)
    masks = [gap == dy - 1 for dy in range(3)]
    for dz in range(3):
        for dx in range(3):
            wides = [
                jnp.dot(weight[9 * dz + 3 * dy + dx], repeat, preferred_element_type=F32) for dy in range(3)
            ]
            for m in range(4):
                cut = slice(128 * m, 128 * m + 128)
                band = jnp.zeros((32, 8, 128), F32)
                for dy in range(3):
                    w = jnp.broadcast_to(wides[dy][:, cut].reshape(32, 1, 128), (32, 8, 128))
                    band = jnp.where(jnp.broadcast_to(masks[dy][None], (32, 8, 128)), w, band)
                out[dx, :, 512 * dz + 128 * m : 512 * dz + 128 * m + 128] = band.reshape(256, 128).astype(BF16)


def spread_filters(where, weight):
    return pl.pallas_call(
        spread_kernel,
        out_shape=jax.ShapeDtypeStruct((3, 256, 1536), BF16),
        in_specs=[smem(), vmem()],
        out_specs=vmem(),
        compiler_params=pltpu.CompilerParams(vmem_limit_bytes=8 * 2**20),
        cost_estimate=pl.CostEstimate(flops=2 * 27 * 256 * 64 * 512, bytes_accessed=2**21, transcendentals=0),
        name="spread_filters",
    )(where, weight)


def input_kernel(where, spread, g_own, g_nbr, g_far, out, stack):
    row, col = where[0], where[1]
    offset = row + col
    lane = iota((256, 128), 1)
    for index in range(-1, 5):
        at = offset + index
        inside = (at >= 0) & (at < 6)
        at = jnp.clip(at, 0, 5)
        parts = [
            g_own[:, 7 * row + 3 * col + at].reshape(128, 128),
            g_nbr[:, 3 * col + at].reshape(128, 128),
            g_far[:, at].reshape(256, 128),
        ]
        for part, first in zip(parts, (0, 128, 256)):
            if index in (-1, 4):
                part = jnp.where(inside, part, jnp.zeros_like(part))
            for dz in range(3):
                z = index + dz - 1
                if 0 <= z < 4:
                    stack[512 * dz + first : 512 * dz + first + part.shape[0], 128 * z : 128 * z + 128] = part
    sums = [jnp.dot(spread[dx], stack[...], preferred_element_type=F32) for dx in range(3)]
    for z in range(4):
        cut = slice(128 * z, 128 * z + 128)
        value = sums[1][:, cut]
        value = value + jnp.where(lane == 127, 0.0, pltpu.roll(sums[0][:, cut], 127, 1))
        value = value + jnp.where(lane == 0, 0.0, pltpu.roll(sums[2][:, cut], 1, 1))
        out[:, z] = value.astype(BF16).reshape(32, 8, 128)


def input_gradient(where, spread, g_own, g_nbr, g_far):
    return pl.pallas_call(
        input_kernel,
        out_shape=jax.ShapeDtypeStruct((32, 4, 8, 128), BF16),
        in_specs=[smem()] + [vmem()] * 4,
        out_specs=vmem(),
        scratch_shapes=[pltpu.VMEM((1536, 512), BF16)],
        compiler_params=pltpu.CompilerParams(vmem_limit_bytes=14 * 2**20),
        cost_estimate=pl.CostEstimate(flops=2 * 9 * 256 * 512 * 512, bytes_accessed=2**22, transcendentals=0),
        name="input_gradient",
    )(where, spread, g_own, g_nbr, g_far)


def swap(block, axis, bits):
    count = lax.axis_size(axis)
    return lax.ppermute(block, axis, [(i, i ^ bits) for i in range(count)])


def line_kernel(chip, two, four, six, after, out):
    out[...] = (chip[...] + two[...]) + (four[...] + six[...])


def line_sum(chip, two, four, six, after):
    return pl.pallas_call(
        line_kernel,
        out_shape=jax.ShapeDtypeStruct(chip.shape, F32),
        in_specs=[vmem()] * 4 + [pl.BlockSpec(memory_space=pl.ANY)],
        out_specs=vmem(),
        compiler_params=pltpu.CompilerParams(vmem_limit_bytes=2**20),
        cost_estimate=pl.CostEstimate(flops=2**16, bytes_accessed=2**18, transcendentals=0),
        name="line_sum",
    )(chip, two, four, six, after)


def slab_kernel(line, across, beside, diagonal, after, out):
    out[0] = line[...] + across[...]
    out[1] = beside[...] + diagonal[...]


def slab_sum(line, across, beside, diagonal, after):
    return pl.pallas_call(
        slab_kernel,
        out_shape=jax.ShapeDtypeStruct((2,) + line.shape, F32),
        in_specs=[vmem()] * 4 + [pl.BlockSpec(memory_space=pl.ANY)],
        out_specs=vmem(),
        compiler_params=pltpu.CompilerParams(vmem_limit_bytes=2**20),
        cost_estimate=pl.CostEstimate(flops=2**16, bytes_accessed=2**18, transcendentals=0),
        name="slab_sum",
    )(line, across, beside, diagonal, after)


def local_grid(activations, grad_out, weight):
    slab = lax.axis_index("slab")
    row, col = slab // 2, slab % 2
    core = lax.axis_index("sample") % 2
    where = jnp.stack([row, col, core]).astype(jnp.int32)
    act = activations[0]
    g_own = grad_out[0]

    a_nbr = swap(act, "slab", 1)
    g_nbr = swap(lax.dynamic_slice_in_dim(g_own, 7 * (1 - row), 9, axis=1), "slab", 2)
    a_rows, g_rows, sums = near_rows(where, g_own, act)
    spread = spread_filters(where, jnp.swapaxes(weight, 1, 2))

    keep, send, g_pass = filter_partial(where, a_rows, g_rows, sums, g_own, g_nbr, a_nbr, spread)
    g_far = swap(g_pass, "slab", 1)
    chip = keep + swap(send, "sample", 1)
    line = line_sum(chip, swap(chip, "sample", 2), swap(chip, "sample", 4), swap(chip, "sample", 6), g_far)
    grad_in = input_gradient(where, spread, g_own, g_nbr, g_far)
    mine = slab_sum(line, swap(line, "slab", 2), swap(line, "slab", 1), swap(line, "slab", 3), grad_in)
    other = swap(mine, "sample", 1)
    cells = 8 * 128 * 4 * lax.axis_size("slab") * lax.axis_size("sample")
    grad_weight, grad_bias = finish(where, mine, other, 1.0 / math.sqrt(cells))
    return grad_in[None], jnp.swapaxes(grad_weight, 1, 2), grad_bias.reshape(64)


def with_halo(block, sides, width):
    for axis, dim in sides:
        count = lax.axis_size(axis)
        forward = [(i, i + 1) for i in range(count - 1)]
        backward = [(target, source) for source, target in forward]
        low = lax.ppermute(
            lax.slice_in_dim(block, block.shape[dim] - width, None, axis=dim), axis, forward
        )
        high = lax.ppermute(lax.slice_in_dim(block, 0, width, axis=dim), axis, backward)
        block = jnp.concatenate([low, block, high], axis=dim)
    return block


def offsets_list():
    return [
        (shift_z, shift_y, shift_x)
        for shift_z in (-1, 0, 1)
        for shift_y in (-1, 0, 1)
        for shift_x in (-1, 0, 1)
    ]


def local_any(activations, grad_out, weight):
    samples, in_chan, planes, y_cells, x_cells = activations.shape
    slabs = lax.axis_size("slab")
    regrouped = lax.all_to_all(grad_out, "slab", split_axis=2, concat_axis=1, tiled=True)
    g_ext = with_halo(regrouped, (("slab", 2),), 1)
    widths = ((0, 0), (0, 0), (0, 0), (1, 1), (1, 1))
    padded_co = jnp.pad(g_ext, widths)
    grad_in = jnp.zeros((samples, in_chan, planes, y_cells, x_cells), F32)
    pieces = []
    for offset, (shift_z, shift_y, shift_x) in enumerate(offsets_list()):
        moved_co = padded_co[
            :,
            :,
            1 - shift_z : 1 - shift_z + planes,
            1 - shift_y : 1 - shift_y + y_cells,
            1 - shift_x : 1 - shift_x + x_cells,
        ]
        pieces.append(jnp.einsum("sozyx,sizyx->oi", moved_co, activations, preferred_element_type=F32))
        grad_in = grad_in + jnp.einsum("oi,sozyx->sizyx", weight[offset], moved_co, preferred_element_type=F32)
    wpart = jnp.stack(pieces)
    bpart = jnp.sum(regrouped.astype(F32), axis=(0, 2, 3, 4))
    wtotal, btotal = lax.psum((wpart, bpart), ("slab", "sample"))
    all_cells = samples * lax.axis_size("sample") * planes * slabs * y_cells * x_cells
    factor = 1.0 / math.sqrt(all_cells)
    return (grad_in.astype(BF16), wtotal * factor, btotal * factor)


def local(activations, grad_out, weight):
    grid = (
        lax.axis_size("slab") == 4
        and lax.axis_size("sample") == 8
        and activations.shape == (1, 32, 4, 8, 128)
        and grad_out.shape == (1, 16, 16, 8, 128)
    )
    return (local_grid if grid else local_any)(activations, grad_out, weight)


def solution(mesh):
    placed = (P("sample", None, "slab", None, None), P("sample", "slab", None, None, None), P())
    return jax.shard_map(
        local,
        mesh=mesh,
        in_specs=placed,
        out_specs=(P("sample", None, "slab", None, None), P(), P()),
        check_vma=False,
    )
```

```python
import functools
import math

import jax
import jax.numpy as jnp
from jax import lax
from jax.experimental import pallas as pl
from jax.experimental.pallas import tpu as pltpu
from jax.sharding import PartitionSpec as P

F32 = jnp.float32
BF16 = jnp.bfloat16
NT = (((1,), (1,)), ((), ()))


def iota(shape, dim):
    return lax.broadcasted_iota(jnp.int32, shape, dim)


def grid_place():
    slab = lax.axis_index("slab")
    return slab // 2, lax.rem(slab, 2), lax.rem(lax.axis_index("sample"), 2)


def vmem():
    return pl.BlockSpec(memory_space=pltpu.VMEM)


def anywhere():
    return pl.BlockSpec(memory_space=pl.ANY)


def one(mask):
    return mask.astype(F32).astype(BF16)


def turn_planes(turned, shift_rows, store):
    pass


def act_rows(source, put):
    r, q = iota((256, 256), 0), iota((256, 256), 1)
    perm = one(((q & 7) == (r >> 5)) & ((q >> 3) == (r & 31)))
    both = jnp.concatenate([source[:, plane].reshape(256, 128) for plane in range(4)], axis=1)
    turned = jnp.dot(perm, both, preferred_element_type=F32).astype(BF16)
    for plane in range(4):
        for y in range(8):
            put(plane, y, turned[32 * y : 32 * y + 32, 128 * plane : 128 * plane + 128])


def cot_rows(source, first, row, put):
    r, q = iota((128, 128), 0), iota((128, 128), 1)
    perm = one(((q & 7) == (r >> 4)) & ((q >> 3) == (r & 15)))
    lane = iota((128, 128), 1)
    total = jnp.zeros((16, 128), F32)
    for plane in range(9):
        turned = jnp.dot(perm, source[:, first + plane].reshape(128, 128), preferred_element_type=F32)
        moved = (
            jnp.where(lane == 127, 0.0, pltpu.roll(turned, 127, 1)),
            turned,
            jnp.where(lane == 0, 0.0, pltpu.roll(turned, 1, 1)),
        )
        for shift in range(3):
            packed = moved[shift].astype(BF16)
            for y in range(8):
                put(plane, shift, y, packed[16 * y : 16 * y + 16])
        cells = turned[0:16]
        for y in range(1, 8):
            cells = cells + turned[16 * y : 16 * y + 16]
        if plane == 0:
            cells = jnp.where(row == 0, cells, 0.0)
        if plane == 8:
            cells = jnp.where(row == 0, 0.0, cells)
        total = total + cells
    return total


def act_put(abuf, first):
    def put(plane, y, piece):
        abuf[first + plane, :, 128 * y + 128 : 128 * y + 256] = piece

    return put


def cot_put(gbuf, row, whose):
    def put(plane, shift, y, piece):
        rows = pl.ds(pl.multiple_of(32 * shift + 16 * whose, 16), 16)
        gbuf[plane + 1 - row, rows, 128 * y : 128 * y + 128] = piece

    return put


def near_kernel(g_own, a_own, abuf, gbuf, sums):
    row, col, _ = grid_place()
    for slot in range(12):
        if slot in (0, 1, 10, 11):
            abuf[slot] = jnp.zeros((32, 1280), BF16)
        else:
            abuf[slot, :, 0:128] = jnp.zeros((32, 128), BF16)
            abuf[slot, :, 1152:1280] = jnp.zeros((32, 128), BF16)
    for slot in range(10):
        gbuf[slot, 96:128] = jnp.zeros((32, 1024), BF16)
    gbuf[9 * row] = jnp.zeros((128, 1024), BF16)
    act_rows(a_own, act_put(abuf, 2 + 4 * col))
    sums[...] = cot_rows(g_own, 7 * row, row, cot_put(gbuf, row, row))


ROWS = (
    jax.ShapeDtypeStruct((12, 32, 1280), BF16),
    jax.ShapeDtypeStruct((10, 128, 1024), BF16),
)


def near_rows(g_own, a_own):
    return pl.pallas_call(
        near_kernel,
        out_shape=ROWS + (jax.ShapeDtypeStruct((16, 128), F32),),
        in_specs=[vmem(), vmem()],
        out_specs=(vmem(), vmem(), vmem()),
        compiler_params=pltpu.CompilerParams(vmem_limit_bytes=10 * 2**20),
        cost_estimate=pl.CostEstimate(flops=2**28, bytes_accessed=2**21, transcendentals=0),
        name="near_rows",
    )(g_own, a_own)


def filter_kernel(a_in, g_in, sums, g_nbr, a_nbr, abuf, gbuf, keep, send):
    row, col, core = grid_place()
    act_rows(a_nbr, act_put(abuf, 6 - 4 * col))
    far_sums = cot_rows(g_nbr, 0, row, cot_put(gbuf, row, 1 - row))
    wide = jnp.zeros((384, 256), F32)
    for slot in range(0, 10, 2):
        moved = [
            abuf[slot + plane, :, 128 * shift : 128 * shift + 1024] for plane in range(4) for shift in range(3)
        ]
        wide = wide + lax.dot_general(
            jnp.concatenate(moved, axis=0),
            gbuf[slot : slot + 2].reshape(256, 1024),
            NT,
            preferred_element_type=F32,
        )
    acc = wide[0:288, 0:128] + wide[96:384, 128:256]
    side = jnp.concatenate([acc[216:288, 32 * m : 32 * m + 32] for m in range(3)], axis=0)
    table = jnp.concatenate([acc[0:216, 0:96], side], axis=1)
    first = jnp.where(row == 0, sums[...], far_sums)
    second = jnp.where(row == 0, far_sums, sums[...])
    column = jnp.sum(jnp.concatenate([first, second], axis=0), axis=1, keepdims=True)
    line = jnp.sum(jnp.where(iota((32, 128), 0) == iota((32, 128), 1), column, 0.0), axis=0, keepdims=True)
    bias = jnp.where(iota((8, 128), 0) == 0, line, 0.0)
    low = table[0:112]
    high = jnp.concatenate([table[112:216], bias], axis=0)
    keep[...] = jnp.where(core == 0, low, high)
    send[...] = jnp.where(core == 0, high, low)


def filter_partial(a_rows, g_rows, sums, g_nbr, a_nbr):
    half = jax.ShapeDtypeStruct((112, 128), F32)
    return pl.pallas_call(
        filter_kernel,
        out_shape=ROWS + (half, half),
        in_specs=[vmem()] * 5,
        out_specs=(vmem(),) * 4,
        input_output_aliases={0: 0, 1: 1},
        compiler_params=pltpu.CompilerParams(vmem_limit_bytes=12 * 2**20),
        cost_estimate=pl.CostEstimate(flops=2 * 10 * 288 * 96 * 1024, bytes_accessed=2**21, transcendentals=0),
        name="filter_partial",
    )(a_rows, g_rows, sums, g_nbr, a_nbr)[2:]


def pass_kernel(g_own, g_nbr, after, out):
    row, col, _ = grid_place()
    for plane in range(6):
        out[0:16, plane] = g_own[:, 7 * row + 3 * (1 - col) + plane]
        out[16:32, plane] = g_nbr[:, 3 * (1 - col) + plane]


def pass_on(g_own, g_nbr, after):
    return pl.pallas_call(
        pass_kernel,
        out_shape=jax.ShapeDtypeStruct((32, 6, 8, 128), BF16),
        in_specs=[vmem(), vmem(), anywhere()],
        out_specs=vmem(),
        compiler_params=pltpu.CompilerParams(vmem_limit_bytes=4 * 2**20),
        cost_estimate=pl.CostEstimate(flops=2**30, bytes_accessed=2**23, transcendentals=0),
        name="pass_on",
    )(g_own, g_nbr, after)


def finish_kernel(factor, mine, other, weight_out, bias_out):
    _, col, core = grid_place()
    lane = iota((224, 128), 1)
    tables = []
    for x in range(2):
        which = jnp.where(col == x, 0, 1)
        a, b = mine[which], other[which]
        low, high = jnp.where(core == 0, a, b), jnp.where(core == 0, b, a)
        tables.append(jnp.concatenate([low, high], axis=0) * factor)
    even = (lane & 16) == 0
    first = jnp.where(even, tables[0], pltpu.roll(tables[1], 16, 1))
    second = jnp.where(even, pltpu.roll(tables[0], 112, 1), tables[1])
    whole = []
    for dx in range(4):
        left = pltpu.roll(first, 128 - 32 * dx, 1) if dx else first
        right = pltpu.roll(second, (160 - 32 * dx) % 128, 1) if dx != 1 else second
        whole.append(jnp.where(lane < 32, left, right))
    for nine in range(9):
        for dx in range(3):
            k = 3 * nine + dx
            if nine < 6:
                weight_out[k] = whole[dx][32 * nine : 32 * nine + 32, 0:64]
            elif nine == 6:
                weight_out[k, 0:24] = whole[dx][192:216, 0:64]
                weight_out[k, 24:32] = whole[3][72 * dx : 72 * dx + 8, 0:64]
            else:
                at = 72 * dx + 32 * nine - 216
                weight_out[k] = whole[3][at : at + 32, 0:64]
    bias_out[...] = whole[0][216:217, 0:64]


def finish(mine, other, factor):
    return pl.pallas_call(
        functools.partial(finish_kernel, factor),
        out_shape=(jax.ShapeDtypeStruct((27, 32, 64), F32), jax.ShapeDtypeStruct((1, 64), F32)),
        in_specs=[vmem(), vmem()],
        out_specs=(vmem(), vmem()),
        compiler_params=pltpu.CompilerParams(vmem_limit_bytes=4 * 2**20),
        cost_estimate=pl.CostEstimate(flops=2**18, bytes_accessed=2**20, transcendentals=0),
        name="filter_finish",
    )(mine, other)


def spread_kernel(weight, after, out):
    place = lax.axis_index("slab")
    column = iota((64, 512), 1)
    block = column >> 7
    partner = jnp.where(block == 0, 0, jnp.where(block == 1, 2, jnp.where(block == 2, 1, 3)))
    slab = jnp.bitwise_xor(partner, place)
    repeat = one(iota((64, 512), 0) == 16 * slab + ((column & 127) >> 3))
    gap = iota((8, 128), 0) - (iota((8, 128), 1) & 7)
    masks = [gap == dy - 1 for dy in range(3)]
    for dz in range(3):
        for dx in range(3):
            wides = [
                jnp.dot(weight[9 * dz + 3 * dy + dx], repeat, preferred_element_type=F32) for dy in range(3)
            ]
            for m in range(4):
                cut = slice(128 * m, 128 * m + 128)
                band = jnp.zeros((32, 8, 128), F32)
                for dy in range(3):
                    w = jnp.broadcast_to(wides[dy][:, cut].reshape(32, 1, 128), (32, 8, 128))
                    band = jnp.where(jnp.broadcast_to(masks[dy][None], (32, 8, 128)), w, band)
                first = 256 * dz + 128 * (m % 2)
                out[m // 2, dx, :, first : first + 128] = band.reshape(256, 128).astype(BF16)


def spread_filters(weight, after):
    return pl.pallas_call(
        spread_kernel,
        out_shape=jax.ShapeDtypeStruct((2, 3, 256, 768), BF16),
        in_specs=[vmem(), anywhere()],
        out_specs=vmem(),
        compiler_params=pltpu.CompilerParams(vmem_limit_bytes=8 * 2**20),
        cost_estimate=pl.CostEstimate(flops=2**33, bytes_accessed=2**25, transcendentals=0),
        name="spread_filters",
    )(weight, after)


def stack_planes(offset, parts, stack):
    for index in range(-1, 5):
        at = offset + index
        inside = (at >= 0) & (at < 6)
        at = jnp.clip(at, 0, 5)
        for source, place, first in parts:
            chans = source.shape[0]
            value = source[:, place + at].reshape(8 * chans, 128)
            if index in (-1, 4):
                value = jnp.where(inside, value, jnp.zeros_like(value))
            for dz in range(3):
                z = index + dz - 1
                if 0 <= z < 4:
                    stack[256 * dz + first : 256 * dz + first + 8 * chans, 128 * z : 128 * z + 128] = value


def banded(spread, half, stack):
    lane = iota((256, 512), 1) & 127
    sums = [jnp.dot(spread[half, dx], stack[...], preferred_element_type=F32) for dx in range(3)]
    left = jnp.concatenate([pltpu.roll(sums[0][:, 128 * z : 128 * z + 128], 127, 1) for z in range(4)], axis=1)
    right = jnp.concatenate([pltpu.roll(sums[2][:, 128 * z : 128 * z + 128], 1, 1) for z in range(4)], axis=1)
    return sums[1] + jnp.where(lane == 127, 0.0, left) + jnp.where(lane == 0, 0.0, right)


def near_input_kernel(spread, g_own, g_nbr, out, stack):
    row, col, _ = grid_place()
    stack_planes(row + col, [(g_own, 7 * row + 3 * col, 0), (g_nbr, 3 * col, 128)], stack)
    out[...] = banded(spread, 0, stack)


def near_input(spread, g_own, g_nbr):
    return pl.pallas_call(
        near_input_kernel,
        out_shape=jax.ShapeDtypeStruct((256, 512), F32),
        in_specs=[vmem()] * 3,
        out_specs=vmem(),
        scratch_shapes=[pltpu.VMEM((768, 512), BF16)],
        compiler_params=pltpu.CompilerParams(vmem_limit_bytes=10 * 2**20),
        cost_estimate=pl.CostEstimate(flops=2**33, bytes_accessed=2**25, transcendentals=0),
        name="near_input",
    )(spread, g_own, g_nbr)


def far_input_kernel(spread, g_far, near, out, mark, stack):
    row, col, _ = grid_place()
    stack_planes(row + col, [(g_far, 0, 0)], stack)
    total = (banded(spread, 1, stack) + near[...]).astype(BF16)
    for z in range(4):
        out[:, z] = total[:, 128 * z : 128 * z + 128].reshape(32, 8, 128)
    mark[...] = jnp.zeros((8, 128), F32)


def far_input(spread, g_far, near):
    return pl.pallas_call(
        far_input_kernel,
        out_shape=(jax.ShapeDtypeStruct((32, 4, 8, 128), BF16), jax.ShapeDtypeStruct((8, 128), F32)),
        in_specs=[vmem()] * 3,
        out_specs=(vmem(), vmem()),
        scratch_shapes=[pltpu.VMEM((768, 512), BF16)],
        compiler_params=pltpu.CompilerParams(vmem_limit_bytes=10 * 2**20),
        cost_estimate=pl.CostEstimate(flops=9 * 256 * 256 * 512, bytes_accessed=2**22, transcendentals=0),
        name="far_input",
    )(spread, g_far, near)


def swap(block, axis, bits):
    count = lax.axis_size(axis)
    return lax.ppermute(block, axis, [(i, i ^ bits) for i in range(count)])


def line_kernel(chip, two, four, six, after, out):
    out[...] = (chip[...] + two[...]) + (four[...] + six[...])


def line_sum(chip, two, four, six, after):
    return pl.pallas_call(
        line_kernel,
        out_shape=jax.ShapeDtypeStruct(chip.shape, F32),
        in_specs=[vmem()] * 4 + [anywhere()],
        out_specs=vmem(),
        compiler_params=pltpu.CompilerParams(vmem_limit_bytes=2**20),
        cost_estimate=pl.CostEstimate(flops=2**16, bytes_accessed=2**18, transcendentals=0),
        name="line_sum",
    )(chip, two, four, six, after)


def slab_kernel(line, across, beside, diagonal, after, out):
    out[0] = line[...] + across[...]
    out[1] = beside[...] + diagonal[...]


def slab_sum(line, across, beside, diagonal, after):
    return pl.pallas_call(
        slab_kernel,
        out_shape=jax.ShapeDtypeStruct((2,) + line.shape, F32),
        in_specs=[vmem()] * 4 + [anywhere()],
        out_specs=vmem(),
        compiler_params=pltpu.CompilerParams(vmem_limit_bytes=2**20),
        cost_estimate=pl.CostEstimate(flops=2**16, bytes_accessed=2**18, transcendentals=0),
        name="slab_sum",
    )(line, across, beside, diagonal, after)


def local_grid(activations, grad_out, weight):
    slab = lax.axis_index("slab")
    row = slab // 2
    act = activations[0]
    g_own = grad_out[0]

    a_nbr = swap(act, "slab", 1)
    g_nbr = swap(lax.dynamic_slice_in_dim(g_own, 7 * (1 - row), 9, axis=1), "slab", 2)
    a_rows, g_rows, sums = near_rows(g_own, act)
    keep, send = filter_partial(a_rows, g_rows, sums, g_nbr, a_nbr)
    chip = keep + swap(send, "sample", 1)
    g_far = swap(pass_on(g_own, g_nbr, keep), "slab", 1)
    spread = spread_filters(jnp.swapaxes(weight, 1, 2), chip)
    near = near_input(spread, g_own, g_nbr)
    line = line_sum(chip, swap(chip, "sample", 2), swap(chip, "sample", 4), swap(chip, "sample", 6), near)
    grad_in, mark = far_input(spread, g_far, near)
    mine = slab_sum(line, swap(line, "slab", 2), swap(line, "slab", 1), swap(line, "slab", 3), mark)
    other = swap(mine, "sample", 1)
    cells = 8 * 128 * 4 * lax.axis_size("slab") * lax.axis_size("sample")
    grad_weight, grad_bias = finish(mine, other, 1.0 / math.sqrt(cells))
    return grad_in[None], jnp.swapaxes(grad_weight, 1, 2), grad_bias.reshape(64)


def with_halo(block, sides, width):
    for axis, dim in sides:
        count = lax.axis_size(axis)
        forward = [(i, i + 1) for i in range(count - 1)]
        backward = [(target, source) for source, target in forward]
        low = lax.ppermute(
            lax.slice_in_dim(block, block.shape[dim] - width, None, axis=dim), axis, forward
        )
        high = lax.ppermute(lax.slice_in_dim(block, 0, width, axis=dim), axis, backward)
        block = jnp.concatenate([low, block, high], axis=dim)
    return block


def offsets_list():
    return [
        (shift_z, shift_y, shift_x)
        for shift_z in (-1, 0, 1)
        for shift_y in (-1, 0, 1)
        for shift_x in (-1, 0, 1)
    ]


def local_any(activations, grad_out, weight):
    samples, in_chan, planes, y_cells, x_cells = activations.shape
    slabs = lax.axis_size("slab")
    regrouped = lax.all_to_all(grad_out, "slab", split_axis=2, concat_axis=1, tiled=True)
    g_ext = with_halo(regrouped, (("slab", 2),), 1)
    widths = ((0, 0), (0, 0), (0, 0), (1, 1), (1, 1))
    padded_co = jnp.pad(g_ext, widths)
    grad_in = jnp.zeros((samples, in_chan, planes, y_cells, x_cells), F32)
    pieces = []
    for offset, (shift_z, shift_y, shift_x) in enumerate(offsets_list()):
        moved_co = padded_co[
            :,
            :,
            1 - shift_z : 1 - shift_z + planes,
            1 - shift_y : 1 - shift_y + y_cells,
            1 - shift_x : 1 - shift_x + x_cells,
        ]
        pieces.append(jnp.einsum("sozyx,sizyx->oi", moved_co, activations, preferred_element_type=F32))
        grad_in = grad_in + jnp.einsum("oi,sozyx->sizyx", weight[offset], moved_co, preferred_element_type=F32)
    wpart = jnp.stack(pieces)
    bpart = jnp.sum(regrouped.astype(F32), axis=(0, 2, 3, 4))
    wtotal, btotal = lax.psum((wpart, bpart), ("slab", "sample"))
    all_cells = samples * lax.axis_size("sample") * planes * slabs * y_cells * x_cells
    factor = 1.0 / math.sqrt(all_cells)
    return (grad_in.astype(BF16), wtotal * factor, btotal * factor)


def local(activations, grad_out, weight):
    grid = (
        lax.axis_size("slab") == 4
        and lax.axis_size("sample") == 8
        and activations.shape == (1, 32, 4, 8, 128)
        and grad_out.shape == (1, 16, 16, 8, 128)
    )
    return (local_grid if grid else local_any)(activations, grad_out, weight)


def solution(mesh):
    placed = (P("sample", None, "slab", None, None), P("sample", "slab", None, None, None), P())
    return jax.shard_map(
        local,
        mesh=mesh,
        in_specs=placed,
        out_specs=(P("sample", None, "slab", None, None), P(), P()),
        check_vma=False,
    )
```

```python
import functools
import math

import jax
import jax.numpy as jnp
from jax import lax
from jax.experimental import pallas as pl
from jax.experimental.pallas import tpu as pltpu
from jax.sharding import PartitionSpec as P

F32 = jnp.float32
BF16 = jnp.bfloat16
NT = (((1,), (1,)), ((), ()))


def iota(shape, dim):
    return lax.broadcasted_iota(jnp.int32, shape, dim)


def grid_place():
    slab = lax.axis_index("slab")
    return slab // 2, lax.rem(slab, 2), lax.rem(lax.axis_index("sample"), 2)


def vmem():
    return pl.BlockSpec(memory_space=pltpu.VMEM)


def anywhere():
    return pl.BlockSpec(memory_space=pl.ANY)


def one(mask):
    return mask.astype(F32).astype(BF16)


def turn_planes(turned, shift_rows, store):
    pass


def act_rows(source, put):
    r, q = iota((256, 256), 0), iota((256, 256), 1)
    perm = one(((q & 7) == (r >> 5)) & ((q >> 3) == (r & 31)))
    both = jnp.concatenate([source[:, plane].reshape(256, 128) for plane in range(4)], axis=1)
    turned = jnp.dot(perm, both, preferred_element_type=F32).astype(BF16)
    for plane in range(4):
        for y in range(8):
            put(plane, y, turned[32 * y : 32 * y + 32, 128 * plane : 128 * plane + 128])


def cot_rows(source, first, row, put):
    r, q = iota((128, 128), 0), iota((128, 128), 1)
    perm = one(((q & 7) == (r >> 4)) & ((q >> 3) == (r & 15)))
    lane = iota((128, 128), 1)
    total = jnp.zeros((16, 128), F32)
    for plane in range(9):
        turned = jnp.dot(perm, source[:, first + plane].reshape(128, 128), preferred_element_type=F32)
        moved = (
            jnp.where(lane == 127, 0.0, pltpu.roll(turned, 127, 1)),
            turned,
            jnp.where(lane == 0, 0.0, pltpu.roll(turned, 1, 1)),
        )
        for shift in range(3):
            packed = moved[shift].astype(BF16)
            for y in range(8):
                put(plane, shift, y, packed[16 * y : 16 * y + 16])
        cells = turned[0:16]
        for y in range(1, 8):
            cells = cells + turned[16 * y : 16 * y + 16]
        if plane == 0:
            cells = jnp.where(row == 0, cells, 0.0)
        if plane == 8:
            cells = jnp.where(row == 0, 0.0, cells)
        total = total + cells
    return total


def act_put(abuf, first):
    def put(plane, y, piece):
        abuf[first + plane, :, 128 * y + 128 : 128 * y + 256] = piece

    return put


def cot_put(gbuf, row, whose):
    def put(plane, shift, y, piece):
        rows = pl.ds(pl.multiple_of(32 * shift + 16 * whose, 16), 16)
        gbuf[plane + 1 - row, rows, 128 * y : 128 * y + 128] = piece

    return put


def near_kernel(g_own, a_own, abuf, gbuf, sums):
    row, col, _ = grid_place()
    for plane in range(8):
        abuf[plane, :, 0:128] = jnp.zeros((32, 128), BF16)
        abuf[plane, :, 1152:1280] = jnp.zeros((32, 128), BF16)
    for slot in range(10):
        gbuf[slot, 96:128] = jnp.zeros((32, 1024), BF16)
    gbuf[9 * row] = jnp.zeros((128, 1024), BF16)
    act_rows(a_own, act_put(abuf, 4 * col))
    sums[...] = cot_rows(g_own, 7 * row, row, cot_put(gbuf, row, row))


ROWS = (
    jax.ShapeDtypeStruct((8, 32, 1280), BF16),
    jax.ShapeDtypeStruct((10, 128, 1024), BF16),
)


def near_rows(g_own, a_own):
    return pl.pallas_call(
        near_kernel,
        out_shape=ROWS + (jax.ShapeDtypeStruct((16, 128), F32),),
        in_specs=[vmem(), vmem()],
        out_specs=(vmem(), vmem(), vmem()),
        compiler_params=pltpu.CompilerParams(vmem_limit_bytes=10 * 2**20),
        cost_estimate=pl.CostEstimate(flops=2**28, bytes_accessed=2**21, transcendentals=0),
        name="near_rows",
    )(g_own, a_own)


def filter_kernel(a_in, g_in, sums, g_nbr, a_nbr, abuf, gbuf, keep, send):
    row, col, core = grid_place()
    act_rows(a_nbr, act_put(abuf, 4 - 4 * col))
    far_sums = cot_rows(g_nbr, 0, row, cot_put(gbuf, row, 1 - row))
    parts = []
    for slot in range(0, 10, 2):
        planes = range(max(slot - 2, 0), min(slot + 2, 8))
        moved = [abuf[plane, :, 128 * shift : 128 * shift + 1024] for plane in planes for shift in range(3)]
        parts.append(
            lax.dot_general(
                jnp.concatenate(moved, axis=0),
                gbuf[slot : slot + 2].reshape(256, 1024),
                NT,
                preferred_element_type=F32,
            )
        )
    whole = parts[1] + parts[2] + parts[3]
    wide = jnp.concatenate([whole[0:192] + parts[4], whole[192:384] + parts[0]], axis=0)
    acc = wide[0:288, 0:128] + wide[96:384, 128:256]
    side = jnp.concatenate([acc[216:288, 32 * m : 32 * m + 32] for m in range(3)], axis=0)
    table = jnp.concatenate([acc[0:216, 0:96], side], axis=1)
    first = jnp.where(row == 0, sums[...], far_sums)
    second = jnp.where(row == 0, far_sums, sums[...])
    column = jnp.sum(jnp.concatenate([first, second], axis=0), axis=1, keepdims=True)
    line = jnp.sum(jnp.where(iota((32, 128), 0) == iota((32, 128), 1), column, 0.0), axis=0, keepdims=True)
    bias = jnp.where(iota((8, 128), 0) == 0, line, 0.0)
    low = table[0:112]
    high = jnp.concatenate([table[112:216], bias], axis=0)
    keep[...] = jnp.where(core == 0, low, high)
    send[...] = jnp.where(core == 0, high, low)


def filter_partial(a_rows, g_rows, sums, g_nbr, a_nbr):
    half = jax.ShapeDtypeStruct((112, 128), F32)
    return pl.pallas_call(
        filter_kernel,
        out_shape=ROWS + (half, half),
        in_specs=[vmem()] * 5,
        out_specs=(vmem(),) * 4,
        input_output_aliases={0: 0, 1: 1},
        compiler_params=pltpu.CompilerParams(vmem_limit_bytes=12 * 2**20),
        cost_estimate=pl.CostEstimate(flops=2 * 10 * 288 * 96 * 1024, bytes_accessed=2**21, transcendentals=0),
        name="filter_partial",
    )(a_rows, g_rows, sums, g_nbr, a_nbr)[2:]


def pass_kernel(g_own, g_nbr, after, out):
    row, col, _ = grid_place()
    for plane in range(6):
        out[0:16, plane] = g_own[:, 7 * row + 3 * (1 - col) + plane]
        out[16:32, plane] = g_nbr[:, 3 * (1 - col) + plane]


def pass_on(g_own, g_nbr, after):
    return pl.pallas_call(
        pass_kernel,
        out_shape=jax.ShapeDtypeStruct((32, 6, 8, 128), BF16),
        in_specs=[vmem(), vmem(), anywhere()],
        out_specs=vmem(),
        compiler_params=pltpu.CompilerParams(vmem_limit_bytes=4 * 2**20),
        cost_estimate=pl.CostEstimate(flops=2**30, bytes_accessed=2**23, transcendentals=0),
        name="pass_on",
    )(g_own, g_nbr, after)


def finish_kernel(factor, mine, other, weight_out, bias_out):
    _, col, core = grid_place()
    lane = iota((224, 128), 1)
    tables = []
    for x in range(2):
        which = jnp.where(col == x, 0, 1)
        a, b = mine[which], other[which]
        low, high = jnp.where(core == 0, a, b), jnp.where(core == 0, b, a)
        tables.append(jnp.concatenate([low, high], axis=0) * factor)
    even = (lane & 16) == 0
    first = jnp.where(even, tables[0], pltpu.roll(tables[1], 16, 1))
    second = jnp.where(even, pltpu.roll(tables[0], 112, 1), tables[1])
    whole = []
    for dx in range(4):
        left = pltpu.roll(first, 128 - 32 * dx, 1) if dx else first
        right = pltpu.roll(second, (160 - 32 * dx) % 128, 1) if dx != 1 else second
        whole.append(jnp.where(lane < 32, left, right))
    for nine in range(9):
        for dx in range(3):
            k = 3 * nine + dx
            if nine < 6:
                weight_out[k] = whole[dx][32 * nine : 32 * nine + 32, 0:64]
            elif nine == 6:
                weight_out[k, 0:24] = whole[dx][192:216, 0:64]
                weight_out[k, 24:32] = whole[3][72 * dx : 72 * dx + 8, 0:64]
            else:
                at = 72 * dx + 32 * nine - 216
                weight_out[k] = whole[3][at : at + 32, 0:64]
    bias_out[...] = whole[0][216:217, 0:64]


def finish(mine, other, factor):
    return pl.pallas_call(
        functools.partial(finish_kernel, factor),
        out_shape=(jax.ShapeDtypeStruct((27, 32, 64), F32), jax.ShapeDtypeStruct((1, 64), F32)),
        in_specs=[vmem(), vmem()],
        out_specs=(vmem(), vmem()),
        compiler_params=pltpu.CompilerParams(vmem_limit_bytes=4 * 2**20),
        cost_estimate=pl.CostEstimate(flops=2**18, bytes_accessed=2**20, transcendentals=0),
        name="filter_finish",
    )(mine, other)


def spread_kernel(weight, after, out):
    place = lax.axis_index("slab")
    column = iota((64, 512), 1)
    block = column >> 7
    partner = jnp.where(block == 0, 0, jnp.where(block == 1, 2, jnp.where(block == 2, 1, 3)))
    slab = jnp.bitwise_xor(partner, place)
    repeat = one(iota((64, 512), 0) == 16 * slab + ((column & 127) >> 3))
    gap = iota((8, 128), 0) - (iota((8, 128), 1) & 7)
    masks = [gap == dy - 1 for dy in range(3)]
    for dz in range(3):
        for dx in range(3):
            wides = [
                jnp.dot(weight[9 * dz + 3 * dy + dx], repeat, preferred_element_type=F32) for dy in range(3)
            ]
            for m in range(4):
                cut = slice(128 * m, 128 * m + 128)
                band = jnp.zeros((32, 8, 128), F32)
                for dy in range(3):
                    w = jnp.broadcast_to(wides[dy][:, cut].reshape(32, 1, 128), (32, 8, 128))
                    band = jnp.where(jnp.broadcast_to(masks[dy][None], (32, 8, 128)), w, band)
                first = 256 * dz + 128 * (m % 2)
                out[m // 2, dx, :, first : first + 128] = band.reshape(256, 128).astype(BF16)


def spread_filters(weight, after):
    return pl.pallas_call(
        spread_kernel,
        out_shape=jax.ShapeDtypeStruct((2, 3, 256, 768), BF16),
        in_specs=[vmem(), anywhere()],
        out_specs=vmem(),
        compiler_params=pltpu.CompilerParams(vmem_limit_bytes=8 * 2**20),
        cost_estimate=pl.CostEstimate(flops=2**33, bytes_accessed=2**25, transcendentals=0),
        name="spread_filters",
    )(weight, after)


def stack_planes(offset, parts, stack):
    for index in range(-1, 5):
        at = offset + index
        inside = (at >= 0) & (at < 6)
        at = jnp.clip(at, 0, 5)
        for source, place, first in parts:
            chans = source.shape[0]
            value = source[:, place + at].reshape(8 * chans, 128)
            if index in (-1, 4):
                value = jnp.where(inside, value, jnp.zeros_like(value))
            for dz in range(3):
                z = index + dz - 1
                if 0 <= z < 4:
                    stack[256 * dz + first : 256 * dz + first + 8 * chans, 128 * z : 128 * z + 128] = value


def banded(spread, half, stack):
    lane = iota((256, 512), 1) & 127
    sums = [jnp.dot(spread[half, dx], stack[...], preferred_element_type=F32) for dx in range(3)]
    left = jnp.concatenate([pltpu.roll(sums[0][:, 128 * z : 128 * z + 128], 127, 1) for z in range(4)], axis=1)
    right = jnp.concatenate([pltpu.roll(sums[2][:, 128 * z : 128 * z + 128], 1, 1) for z in range(4)], axis=1)
    return sums[1] + jnp.where(lane == 127, 0.0, left) + jnp.where(lane == 0, 0.0, right)


def near_input_kernel(spread, g_own, g_nbr, out, stack):
    row, col, _ = grid_place()
    stack_planes(row + col, [(g_own, 7 * row + 3 * col, 0), (g_nbr, 3 * col, 128)], stack)
    out[...] = banded(spread, 0, stack)


def near_input(spread, g_own, g_nbr):
    return pl.pallas_call(
        near_input_kernel,
        out_shape=jax.ShapeDtypeStruct((256, 512), F32),
        in_specs=[vmem()] * 3,
        out_specs=vmem(),
        scratch_shapes=[pltpu.VMEM((768, 512), BF16)],
        compiler_params=pltpu.CompilerParams(vmem_limit_bytes=10 * 2**20),
        cost_estimate=pl.CostEstimate(flops=2**33, bytes_accessed=2**25, transcendentals=0),
        name="near_input",
    )(spread, g_own, g_nbr)


def far_input_kernel(spread, g_far, near, out, mark, stack):
    row, col, _ = grid_place()
    stack_planes(row + col, [(g_far, 0, 0)], stack)
    total = (banded(spread, 1, stack) + near[...]).astype(BF16)
    for z in range(4):
        out[:, z] = total[:, 128 * z : 128 * z + 128].reshape(32, 8, 128)
    mark[...] = jnp.zeros((8, 128), F32)


def far_input(spread, g_far, near):
    return pl.pallas_call(
        far_input_kernel,
        out_shape=(jax.ShapeDtypeStruct((32, 4, 8, 128), BF16), jax.ShapeDtypeStruct((8, 128), F32)),
        in_specs=[vmem()] * 3,
        out_specs=(vmem(), vmem()),
        scratch_shapes=[pltpu.VMEM((768, 512), BF16)],
        compiler_params=pltpu.CompilerParams(vmem_limit_bytes=10 * 2**20),
        cost_estimate=pl.CostEstimate(flops=9 * 256 * 256 * 512, bytes_accessed=2**22, transcendentals=0),
        name="far_input",
    )(spread, g_far, near)


def swap(block, axis, bits):
    count = lax.axis_size(axis)
    return lax.ppermute(block, axis, [(i, i ^ bits) for i in range(count)])


def line_kernel(chip, two, six, four, after, out):
    out[...] = (chip[...] + two[...]) + (four[...] + six[...])


def line_sum(chip, two, six, four, after):
    return pl.pallas_call(
        line_kernel,
        out_shape=jax.ShapeDtypeStruct(chip.shape, F32),
        in_specs=[vmem()] * 4 + [anywhere()],
        out_specs=vmem(),
        compiler_params=pltpu.CompilerParams(vmem_limit_bytes=2**20),
        cost_estimate=pl.CostEstimate(flops=2**16, bytes_accessed=2**18, transcendentals=0),
        name="line_sum",
    )(chip, two, six, four, after)


def slab_kernel(line, across, beside, diagonal, after, out):
    out[0] = line[...] + across[...]
    out[1] = beside[...] + diagonal[...]


def slab_sum(line, across, beside, diagonal, after):
    return pl.pallas_call(
        slab_kernel,
        out_shape=jax.ShapeDtypeStruct((2,) + line.shape, F32),
        in_specs=[vmem()] * 4 + [anywhere()],
        out_specs=vmem(),
        compiler_params=pltpu.CompilerParams(vmem_limit_bytes=2**20),
        cost_estimate=pl.CostEstimate(flops=2**16, bytes_accessed=2**18, transcendentals=0),
        name="slab_sum",
    )(line, across, beside, diagonal, after)


def local_grid(activations, grad_out, weight):
    slab = lax.axis_index("slab")
    row = slab // 2
    act = activations[0]
    g_own = grad_out[0]

    a_nbr = swap(act, "slab", 1)
    g_nbr = swap(lax.dynamic_slice_in_dim(g_own, 7 * (1 - row), 9, axis=1), "slab", 2)
    a_rows, g_rows, sums = near_rows(g_own, act)
    keep, send = filter_partial(a_rows, g_rows, sums, g_nbr, a_nbr)
    chip = keep + swap(send, "sample", 1)
    g_far = swap(pass_on(g_own, g_nbr, keep), "slab", 1)
    spread = spread_filters(jnp.swapaxes(weight, 1, 2), chip)
    near = near_input(spread, g_own, g_nbr)
    line = line_sum(chip, swap(chip, "sample", 2), swap(chip, "sample", 6), swap(chip, "sample", 4), near)
    grad_in, mark = far_input(spread, g_far, near)
    mine = slab_sum(line, swap(line, "slab", 2), swap(line, "slab", 1), swap(line, "slab", 3), mark)
    other = swap(mine, "sample", 1)
    cells = 8 * 128 * 4 * lax.axis_size("slab") * lax.axis_size("sample")
    grad_weight, grad_bias = finish(mine, other, 1.0 / math.sqrt(cells))
    return grad_in[None], jnp.swapaxes(grad_weight, 1, 2), grad_bias.reshape(64)


def with_halo(block, sides, width):
    for axis, dim in sides:
        count = lax.axis_size(axis)
        forward = [(i, i + 1) for i in range(count - 1)]
        backward = [(target, source) for source, target in forward]
        low = lax.ppermute(
            lax.slice_in_dim(block, block.shape[dim] - width, None, axis=dim), axis, forward
        )
        high = lax.ppermute(lax.slice_in_dim(block, 0, width, axis=dim), axis, backward)
        block = jnp.concatenate([low, block, high], axis=dim)
    return block


def offsets_list():
    return [
        (shift_z, shift_y, shift_x)
        for shift_z in (-1, 0, 1)
        for shift_y in (-1, 0, 1)
        for shift_x in (-1, 0, 1)
    ]


def local_any(activations, grad_out, weight):
    samples, in_chan, planes, y_cells, x_cells = activations.shape
    slabs = lax.axis_size("slab")
    regrouped = lax.all_to_all(grad_out, "slab", split_axis=2, concat_axis=1, tiled=True)
    g_ext = with_halo(regrouped, (("slab", 2),), 1)
    widths = ((0, 0), (0, 0), (0, 0), (1, 1), (1, 1))
    padded_co = jnp.pad(g_ext, widths)
    grad_in = jnp.zeros((samples, in_chan, planes, y_cells, x_cells), F32)
    pieces = []
    for offset, (shift_z, shift_y, shift_x) in enumerate(offsets_list()):
        moved_co = padded_co[
            :,
            :,
            1 - shift_z : 1 - shift_z + planes,
            1 - shift_y : 1 - shift_y + y_cells,
            1 - shift_x : 1 - shift_x + x_cells,
        ]
        pieces.append(jnp.einsum("sozyx,sizyx->oi", moved_co, activations, preferred_element_type=F32))
        grad_in = grad_in + jnp.einsum("oi,sozyx->sizyx", weight[offset], moved_co, preferred_element_type=F32)
    wpart = jnp.stack(pieces)
    bpart = jnp.sum(regrouped.astype(F32), axis=(0, 2, 3, 4))
    wtotal, btotal = lax.psum((wpart, bpart), ("slab", "sample"))
    all_cells = samples * lax.axis_size("sample") * planes * slabs * y_cells * x_cells
    factor = 1.0 / math.sqrt(all_cells)
    return (grad_in.astype(BF16), wtotal * factor, btotal * factor)


def local(activations, grad_out, weight):
    grid = (
        lax.axis_size("slab") == 4
        and lax.axis_size("sample") == 8
        and activations.shape == (1, 32, 4, 8, 128)
        and grad_out.shape == (1, 16, 16, 8, 128)
    )
    return (local_grid if grid else local_any)(activations, grad_out, weight)


def solution(mesh):
    placed = (P("sample", None, "slab", None, None), P("sample", "slab", None, None, None), P())
    return jax.shard_map(
        local,
        mesh=mesh,
        in_specs=placed,
        out_specs=(P("sample", None, "slab", None, None), P(), P()),
        check_vma=False,
    )
```

```python
import functools
import math

import jax
import jax.numpy as jnp
from jax import lax
from jax.experimental import pallas as pl
from jax.experimental.pallas import tpu as pltpu
from jax.sharding import PartitionSpec as P

F32 = jnp.float32
BF16 = jnp.bfloat16
NT = (((1,), (1,)), ((), ()))


def iota(shape, dim):
    return lax.broadcasted_iota(jnp.int32, shape, dim)


def grid_place():
    slab = lax.axis_index("slab")
    return slab // 2, lax.rem(slab, 2), lax.rem(lax.axis_index("sample"), 2)


def vmem():
    return pl.BlockSpec(memory_space=pltpu.VMEM)


def anywhere():
    return pl.BlockSpec(memory_space=pl.ANY)


def one(mask):
    return mask.astype(F32).astype(BF16)


def turn_planes(turned, shift_rows, store):
    pass


def act_rows(source, put):
    r, q = iota((256, 256), 0), iota((256, 256), 1)
    perm = one(((q & 7) == (r >> 5)) & ((q >> 3) == (r & 31)))
    both = jnp.concatenate([source[:, plane].reshape(256, 128) for plane in range(4)], axis=1)
    turned = jnp.dot(perm, both, preferred_element_type=F32).astype(BF16)
    for plane in range(4):
        for y in range(8):
            put(plane, y, turned[32 * y : 32 * y + 32, 128 * plane : 128 * plane + 128])


def cot_rows(source, first, row, put):
    r, q = iota((128, 128), 0), iota((128, 128), 1)
    perm = one(((q & 7) == (r >> 4)) & ((q >> 3) == (r & 15)))
    lane = iota((128, 128), 1)
    total = jnp.zeros((16, 128), F32)
    for plane in range(9):
        turned = jnp.dot(perm, source[:, first + plane].reshape(128, 128), preferred_element_type=F32)
        moved = (
            jnp.where(lane == 127, 0.0, pltpu.roll(turned, 127, 1)),
            turned,
            jnp.where(lane == 0, 0.0, pltpu.roll(turned, 1, 1)),
        )
        for shift in range(3):
            packed = moved[shift].astype(BF16)
            for y in range(8):
                put(plane, shift, y, packed[16 * y : 16 * y + 16])
        cells = turned[0:16]
        for y in range(1, 8):
            cells = cells + turned[16 * y : 16 * y + 16]
        if plane == 0:
            cells = jnp.where(row == 0, cells, 0.0)
        if plane == 8:
            cells = jnp.where(row == 0, 0.0, cells)
        total = total + cells
    return total


def act_put(abuf, first):
    def put(plane, y, piece):
        abuf[first + plane, :, 128 * y + 128 : 128 * y + 256] = piece

    return put


def cot_put(gbuf, row, whose):
    def put(plane, shift, y, piece):
        rows = pl.ds(pl.multiple_of(32 * shift + 16 * whose, 16), 16)
        gbuf[plane + 1 - row, rows, 128 * y : 128 * y + 128] = piece

    return put


def near_kernel(g_own, a_own, abuf, gbuf, sums):
    row, col, _ = grid_place()
    for plane in range(8):
        abuf[plane, :, 0:128] = jnp.zeros((32, 128), BF16)
        abuf[plane, :, 1152:1280] = jnp.zeros((32, 128), BF16)
    for slot in range(10):
        gbuf[slot, 96:128] = jnp.zeros((32, 1024), BF16)
    gbuf[9 * row] = jnp.zeros((128, 1024), BF16)
    act_rows(a_own, act_put(abuf, 4 * col))
    sums[...] = cot_rows(g_own, 7 * row, row, cot_put(gbuf, row, row))


ROWS = (
    jax.ShapeDtypeStruct((8, 32, 1280), BF16),
    jax.ShapeDtypeStruct((10, 128, 1024), BF16),
)


def near_rows(g_own, a_own):
    return pl.pallas_call(
        near_kernel,
        out_shape=ROWS + (jax.ShapeDtypeStruct((16, 128), F32),),
        in_specs=[vmem(), vmem()],
        out_specs=(vmem(), vmem(), vmem()),
        compiler_params=pltpu.CompilerParams(vmem_limit_bytes=10 * 2**20),
        cost_estimate=pl.CostEstimate(flops=2**28, bytes_accessed=2**21, transcendentals=0),
        name="near_rows",
    )(g_own, a_own)


def filter_body(row, col, core, sums, g_nbr, a_nbr, abuf, gbuf, keep, send):
    act_rows(a_nbr, act_put(abuf, 4 - 4 * col))
    far_sums = cot_rows(g_nbr, 0, row, cot_put(gbuf, row, 1 - row))
    parts = []
    for slot in range(0, 10, 2):
        planes = range(max(slot - 2, 0), min(slot + 2, 8))
        moved = [abuf[plane, :, 128 * shift : 128 * shift + 1024] for plane in planes for shift in range(3)]
        parts.append(
            lax.dot_general(
                jnp.concatenate(moved, axis=0),
                gbuf[slot : slot + 2].reshape(256, 1024),
                NT,
                preferred_element_type=F32,
            )
        )
    whole = parts[1] + parts[2] + parts[3]
    wide = jnp.concatenate([whole[0:192] + parts[4], whole[192:384] + parts[0]], axis=0)
    acc = wide[0:288, 0:128] + wide[96:384, 128:256]
    side = jnp.concatenate([acc[216:288, 32 * m : 32 * m + 32] for m in range(3)], axis=0)
    table = jnp.concatenate([acc[0:216, 0:96], side], axis=1)
    first = jnp.where(row == 0, sums[...], far_sums)
    second = jnp.where(row == 0, far_sums, sums[...])
    column = jnp.sum(jnp.concatenate([first, second], axis=0), axis=1, keepdims=True)
    line = jnp.sum(jnp.where(iota((32, 128), 0) == iota((32, 128), 1), column, 0.0), axis=0, keepdims=True)
    bias = jnp.where(iota((8, 128), 0) == 0, line, 0.0)
    low = table[0:112]
    high = jnp.concatenate([table[112:216], bias], axis=0)
    keep[...] = jnp.where(core == 0, low, high)
    send[...] = jnp.where(core == 0, high, low)


def filter_kernel(a_in, g_in, sums, g_nbr, a_nbr, after, *outs):
    row, col, core = grid_place()
    for r in range(2):
        for c in range(2):
            pl.when((row == r) & (col == c))(
                functools.partial(filter_body, r, c, core, sums, g_nbr, a_nbr, *outs)
            )


def filter_partial(a_rows, g_rows, sums, g_nbr, a_nbr, after):
    half = jax.ShapeDtypeStruct((112, 128), F32)
    return pl.pallas_call(
        filter_kernel,
        out_shape=ROWS + (half, half),
        in_specs=[vmem()] * 5 + [anywhere()],
        out_specs=(vmem(),) * 4,
        input_output_aliases={0: 0, 1: 1},
        compiler_params=pltpu.CompilerParams(vmem_limit_bytes=12 * 2**20),
        cost_estimate=pl.CostEstimate(flops=2 * 10 * 288 * 96 * 1024, bytes_accessed=2**21, transcendentals=0),
        name="filter_partial",
    )(a_rows, g_rows, sums, g_nbr, a_nbr, after)[2:]


def pass_kernel(g_own, g_nbr, after, out):
    row, col, _ = grid_place()
    for plane in range(6):
        out[0:16, plane] = g_own[:, 7 * row + 3 * (1 - col) + plane]
        out[16:32, plane] = g_nbr[:, 3 * (1 - col) + plane]


def pass_on(g_own, g_nbr, after):
    return pl.pallas_call(
        pass_kernel,
        out_shape=jax.ShapeDtypeStruct((32, 6, 8, 128), BF16),
        in_specs=[vmem(), vmem(), anywhere()],
        out_specs=vmem(),
        compiler_params=pltpu.CompilerParams(vmem_limit_bytes=4 * 2**20),
        cost_estimate=pl.CostEstimate(flops=2**30, bytes_accessed=2**23, transcendentals=0),
        name="pass_on",
    )(g_own, g_nbr, after)


def finish_kernel(factor, mine, other, weight_out, bias_out):
    _, col, core = grid_place()
    lane = iota((224, 128), 1)
    tables = []
    for x in range(2):
        which = jnp.where(col == x, 0, 1)
        a, b = mine[which], other[which]
        low, high = jnp.where(core == 0, a, b), jnp.where(core == 0, b, a)
        tables.append(jnp.concatenate([low, high], axis=0) * factor)
    even = (lane & 16) == 0
    first = jnp.where(even, tables[0], pltpu.roll(tables[1], 16, 1))
    second = jnp.where(even, pltpu.roll(tables[0], 112, 1), tables[1])
    whole = []
    for dx in range(4):
        left = pltpu.roll(first, 128 - 32 * dx, 1) if dx else first
        right = pltpu.roll(second, (160 - 32 * dx) % 128, 1) if dx != 1 else second
        whole.append(jnp.where(lane < 32, left, right))
    for nine in range(9):
        for dx in range(3):
            k = 3 * nine + dx
            if nine < 6:
                weight_out[k] = whole[dx][32 * nine : 32 * nine + 32, 0:64]
            elif nine == 6:
                weight_out[k, 0:24] = whole[dx][192:216, 0:64]
                weight_out[k, 24:32] = whole[3][72 * dx : 72 * dx + 8, 0:64]
            else:
                at = 72 * dx + 32 * nine - 216
                weight_out[k] = whole[3][at : at + 32, 0:64]
    bias_out[...] = whole[0][216:217, 0:64]


def finish(mine, other, factor):
    return pl.pallas_call(
        functools.partial(finish_kernel, factor),
        out_shape=(jax.ShapeDtypeStruct((27, 32, 64), F32), jax.ShapeDtypeStruct((1, 64), F32)),
        in_specs=[vmem(), vmem()],
        out_specs=(vmem(), vmem()),
        compiler_params=pltpu.CompilerParams(vmem_limit_bytes=4 * 2**20),
        cost_estimate=pl.CostEstimate(flops=2**18, bytes_accessed=2**20, transcendentals=0),
        name="filter_finish",
    )(mine, other)


def spread_kernel(weight, after, out):
    place = lax.axis_index("slab")
    column = iota((64, 512), 1)
    block = column >> 7
    partner = jnp.where(block == 0, 0, jnp.where(block == 1, 2, jnp.where(block == 2, 1, 3)))
    slab = jnp.bitwise_xor(partner, place)
    repeat = one(iota((64, 512), 0) == 16 * slab + ((column & 127) >> 3))
    gap = iota((8, 128), 0) - (iota((8, 128), 1) & 7)
    masks = [gap == dy - 1 for dy in range(3)]
    for dz in range(3):
        for dx in range(3):
            wides = [
                jnp.dot(weight[9 * dz + 3 * dy + dx], repeat, preferred_element_type=F32) for dy in range(3)
            ]
            for m in range(4):
                cut = slice(128 * m, 128 * m + 128)
                band = jnp.zeros((32, 8, 128), F32)
                for dy in range(3):
                    w = jnp.broadcast_to(wides[dy][:, cut].reshape(32, 1, 128), (32, 8, 128))
                    band = jnp.where(jnp.broadcast_to(masks[dy][None], (32, 8, 128)), w, band)
                first = 256 * dz + 128 * (m % 2)
                out[m // 2, dx, :, first : first + 128] = band.reshape(256, 128).astype(BF16)


def spread_filters(weight, after):
    return pl.pallas_call(
        spread_kernel,
        out_shape=jax.ShapeDtypeStruct((2, 3, 256, 768), BF16),
        in_specs=[vmem(), anywhere()],
        out_specs=vmem(),
        compiler_params=pltpu.CompilerParams(vmem_limit_bytes=8 * 2**20),
        cost_estimate=pl.CostEstimate(flops=2 * 27 * 256 * 64 * 512, bytes_accessed=2**21, transcendentals=0),
        name="spread_filters",
    )(weight, after)


def stack_planes(offset, parts, stack):
    for index in range(-1, 5):
        at = offset + index
        inside = (at >= 0) & (at < 6)
        at = jnp.clip(at, 0, 5)
        for source, place, first in parts:
            chans = source.shape[0]
            value = source[:, place + at].reshape(8 * chans, 128)
            if index in (-1, 4):
                value = jnp.where(inside, value, jnp.zeros_like(value))
            for dz in range(3):
                z = index + dz - 1
                if 0 <= z < 4:
                    stack[256 * dz + first : 256 * dz + first + 8 * chans, 128 * z : 128 * z + 128] = value


def banded(spread, half, stack):
    lane = iota((256, 512), 1) & 127
    sums = [jnp.dot(spread[half, dx], stack[...], preferred_element_type=F32) for dx in range(3)]
    left = jnp.concatenate([pltpu.roll(sums[0][:, 128 * z : 128 * z + 128], 127, 1) for z in range(4)], axis=1)
    right = jnp.concatenate([pltpu.roll(sums[2][:, 128 * z : 128 * z + 128], 1, 1) for z in range(4)], axis=1)
    return sums[1] + jnp.where(lane == 127, 0.0, left) + jnp.where(lane == 0, 0.0, right)


def near_input_kernel(spread, g_own, g_nbr, out, stack):
    row, col, _ = grid_place()
    stack_planes(row + col, [(g_own, 7 * row + 3 * col, 0), (g_nbr, 3 * col, 128)], stack)
    out[...] = banded(spread, 0, stack)


def near_input(spread, g_own, g_nbr):
    return pl.pallas_call(
        near_input_kernel,
        out_shape=jax.ShapeDtypeStruct((256, 512), F32),
        in_specs=[vmem()] * 3,
        out_specs=vmem(),
        scratch_shapes=[pltpu.VMEM((768, 512), BF16)],
        compiler_params=pltpu.CompilerParams(vmem_limit_bytes=10 * 2**20),
        cost_estimate=pl.CostEstimate(flops=2**33, bytes_accessed=2**25, transcendentals=0),
        name="near_input",
    )(spread, g_own, g_nbr)


def far_input_kernel(spread, g_far, near, out, mark, stack):
    row, col, _ = grid_place()
    stack_planes(row + col, [(g_far, 0, 0)], stack)
    total = (banded(spread, 1, stack) + near[...]).astype(BF16)
    for z in range(4):
        out[:, z] = total[:, 128 * z : 128 * z + 128].reshape(32, 8, 128)
    mark[...] = jnp.zeros((8, 128), F32)


def far_input(spread, g_far, near):
    return pl.pallas_call(
        far_input_kernel,
        out_shape=(jax.ShapeDtypeStruct((32, 4, 8, 128), BF16), jax.ShapeDtypeStruct((8, 128), F32)),
        in_specs=[vmem()] * 3,
        out_specs=(vmem(), vmem()),
        scratch_shapes=[pltpu.VMEM((768, 512), BF16)],
        compiler_params=pltpu.CompilerParams(vmem_limit_bytes=10 * 2**20),
        cost_estimate=pl.CostEstimate(flops=9 * 256 * 256 * 512, bytes_accessed=2**22, transcendentals=0),
        name="far_input",
    )(spread, g_far, near)


def swap(block, axis, bits):
    count = lax.axis_size(axis)
    return lax.ppermute(block, axis, [(i, i ^ bits) for i in range(count)])


def line_kernel(chip, one_off, two_off, both_off, after, out):
    out[...] = (chip[...] + one_off[...]) + (two_off[...] + both_off[...])


def line_sum(chip, one_off, two_off, both_off, after):
    return pl.pallas_call(
        line_kernel,
        out_shape=jax.ShapeDtypeStruct(chip.shape, F32),
        in_specs=[vmem()] * 4 + [anywhere()],
        out_specs=vmem(),
        compiler_params=pltpu.CompilerParams(vmem_limit_bytes=2**20),
        cost_estimate=pl.CostEstimate(flops=2**16, bytes_accessed=2**18, transcendentals=0),
        name="line_sum",
    )(chip, one_off, two_off, both_off, after)


def last_kernel(line, beside, across, diagonal, after, out):
    out[0] = line[...] + across[...]
    out[1] = beside[...] + diagonal[...]


def last_sum(line, beside, across, diagonal, after):
    return pl.pallas_call(
        last_kernel,
        out_shape=jax.ShapeDtypeStruct((2,) + line.shape, F32),
        in_specs=[vmem()] * 4 + [anywhere()],
        out_specs=vmem(),
        compiler_params=pltpu.CompilerParams(vmem_limit_bytes=2**20),
        cost_estimate=pl.CostEstimate(flops=2**16, bytes_accessed=2**18, transcendentals=0),
        name="last_sum",
    )(line, beside, across, diagonal, after)


def swap_at(block, slab_bits, sample_bits):
    count, samples = lax.axis_size(("slab", "sample")), lax.axis_size("sample")
    pairs = [(i, i ^ (samples * slab_bits + sample_bits)) for i in range(count)]
    return lax.ppermute(block, ("slab", "sample"), pairs)


def local_grid(activations, grad_out, weight):
    slab = lax.axis_index("slab")
    row = slab // 2
    act = activations[0]
    g_own = grad_out[0]

    a_nbr = swap(act, "slab", 1)
    g_nbr = swap(lax.dynamic_slice_in_dim(g_own, 7 * (1 - row), 9, axis=1), "slab", 2)
    a_rows, g_rows, sums = near_rows(g_own, act)
    spread = spread_filters(jnp.swapaxes(weight, 1, 2), sums)
    keep, send = filter_partial(a_rows, g_rows, sums, g_nbr, a_nbr, spread)
    chip = keep + swap(send, "sample", 1)
    g_far = swap(pass_on(g_own, g_nbr, keep), "slab", 1)
    near = near_input(spread, g_own, g_nbr)
    line = line_sum(chip, swap_at(chip, 2, 0), swap_at(chip, 0, 2), swap_at(chip, 2, 2), near)
    grad_in, mark = far_input(spread, g_far, near)
    mine = last_sum(line, swap_at(line, 1, 0), swap_at(line, 0, 4), swap_at(line, 1, 4), mark)
    other = swap(mine, "sample", 1)
    cells = 8 * 128 * 4 * lax.axis_size("slab") * lax.axis_size("sample")
    grad_weight, grad_bias = finish(mine, other, 1.0 / math.sqrt(cells))
    return grad_in[None], jnp.swapaxes(grad_weight, 1, 2), grad_bias.reshape(64)


def with_halo(block, sides, width):
    for axis, dim in sides:
        count = lax.axis_size(axis)
        forward = [(i, i + 1) for i in range(count - 1)]
        backward = [(target, source) for source, target in forward]
        low = lax.ppermute(
            lax.slice_in_dim(block, block.shape[dim] - width, None, axis=dim), axis, forward
        )
        high = lax.ppermute(lax.slice_in_dim(block, 0, width, axis=dim), axis, backward)
        block = jnp.concatenate([low, block, high], axis=dim)
    return block


def offsets_list():
    return [
        (shift_z, shift_y, shift_x)
        for shift_z in (-1, 0, 1)
        for shift_y in (-1, 0, 1)
        for shift_x in (-1, 0, 1)
    ]


def local_any(activations, grad_out, weight):
    samples, in_chan, planes, y_cells, x_cells = activations.shape
    slabs = lax.axis_size("slab")
    regrouped = lax.all_to_all(grad_out, "slab", split_axis=2, concat_axis=1, tiled=True)
    g_ext = with_halo(regrouped, (("slab", 2),), 1)
    widths = ((0, 0), (0, 0), (0, 0), (1, 1), (1, 1))
    padded_co = jnp.pad(g_ext, widths)
    grad_in = jnp.zeros((samples, in_chan, planes, y_cells, x_cells), F32)
    pieces = []
    for offset, (shift_z, shift_y, shift_x) in enumerate(offsets_list()):
        moved_co = padded_co[
            :,
            :,
            1 - shift_z : 1 - shift_z + planes,
            1 - shift_y : 1 - shift_y + y_cells,
            1 - shift_x : 1 - shift_x + x_cells,
        ]
        pieces.append(jnp.einsum("sozyx,sizyx->oi", moved_co, activations, preferred_element_type=F32))
        grad_in = grad_in + jnp.einsum("oi,sozyx->sizyx", weight[offset], moved_co, preferred_element_type=F32)
    wpart = jnp.stack(pieces)
    bpart = jnp.sum(regrouped.astype(F32), axis=(0, 2, 3, 4))
    wtotal, btotal = lax.psum((wpart, bpart), ("slab", "sample"))
    all_cells = samples * lax.axis_size("sample") * planes * slabs * y_cells * x_cells
    factor = 1.0 / math.sqrt(all_cells)
    return (grad_in.astype(BF16), wtotal * factor, btotal * factor)


def local(activations, grad_out, weight):
    grid = (
        lax.axis_size("slab") == 4
        and lax.axis_size("sample") == 8
        and activations.shape == (1, 32, 4, 8, 128)
        and grad_out.shape == (1, 16, 16, 8, 128)
    )
    return (local_grid if grid else local_any)(activations, grad_out, weight)


def solution(mesh):
    placed = (P("sample", None, "slab", None, None), P("sample", "slab", None, None, None), P())
    return jax.shard_map(
        local,
        mesh=mesh,
        in_specs=placed,
        out_specs=(P("sample", None, "slab", None, None), P(), P()),
        check_vma=False,
    )
```

```python
import functools
import math

import jax
import jax.numpy as jnp
from jax import lax
from jax.experimental import pallas as pl
from jax.experimental.pallas import tpu as pltpu
from jax.sharding import PartitionSpec as P

F32 = jnp.float32
BF16 = jnp.bfloat16
NT = (((1,), (1,)), ((), ()))


def iota(shape, dim):
    return lax.broadcasted_iota(jnp.int32, shape, dim)


def grid_place():
    slab = lax.axis_index("slab")
    return slab // 2, lax.rem(slab, 2), lax.rem(lax.axis_index("sample"), 2)


def vmem():
    return pl.BlockSpec(memory_space=pltpu.VMEM)


def anywhere():
    return pl.BlockSpec(memory_space=pl.ANY)


def one(mask):
    return mask.astype(F32).astype(BF16)


def turn_planes(turned, shift_rows, store):
    pass


def act_rows(source, put):
    r, q = iota((256, 256), 0), iota((256, 256), 1)
    perm = one(((q & 7) == (r >> 5)) & ((q >> 3) == (r & 31)))
    both = jnp.concatenate([source[:, plane].reshape(256, 128) for plane in range(4)], axis=1)
    turned = jnp.dot(perm, both, preferred_element_type=F32).astype(BF16)
    for plane in range(4):
        for y in range(8):
            put(plane, y, turned[32 * y : 32 * y + 32, 128 * plane : 128 * plane + 128])


def cot_rows(source, first, row, put):
    r, q = iota((128, 128), 0), iota((128, 128), 1)
    perm = one(((q & 7) == (r >> 4)) & ((q >> 3) == (r & 15)))
    lane = iota((128, 128), 1)
    total = jnp.zeros((16, 128), F32)
    for plane in range(9):
        turned = jnp.dot(perm, source[:, first + plane].reshape(128, 128), preferred_element_type=F32)
        moved = (
            jnp.where(lane == 127, 0.0, pltpu.roll(turned, 127, 1)),
            turned,
            jnp.where(lane == 0, 0.0, pltpu.roll(turned, 1, 1)),
        )
        for shift in range(3):
            packed = moved[shift].astype(BF16)
            for y in range(8):
                put(plane, shift, y, packed[16 * y : 16 * y + 16])
        cells = turned[0:16]
        for y in range(1, 8):
            cells = cells + turned[16 * y : 16 * y + 16]
        if plane == 0:
            cells = jnp.where(row == 0, cells, 0.0)
        if plane == 8:
            cells = jnp.where(row == 0, 0.0, cells)
        total = total + cells
    return total


def act_put(abuf, first):
    def put(plane, y, piece):
        abuf[first + plane, :, 128 * y + 128 : 128 * y + 256] = piece

    return put


def cot_put(gbuf, row, whose):
    def put(plane, shift, y, piece):
        rows = pl.ds(pl.multiple_of(32 * shift + 16 * whose, 16), 16)
        gbuf[plane + 1 - row, rows, 128 * y : 128 * y + 128] = piece

    return put


def near_kernel(g_own, a_own, abuf, gbuf, sums):
    row, col, _ = grid_place()
    for plane in range(8):
        abuf[plane, :, 0:128] = jnp.zeros((32, 128), BF16)
        abuf[plane, :, 1152:1280] = jnp.zeros((32, 128), BF16)
    for slot in range(10):
        gbuf[slot, 96:128] = jnp.zeros((32, 1024), BF16)
    gbuf[9 * row] = jnp.zeros((128, 1024), BF16)
    act_rows(a_own, act_put(abuf, 4 * col))
    sums[...] = cot_rows(g_own, 7 * row, row, cot_put(gbuf, row, row))


ROWS = (
    jax.ShapeDtypeStruct((8, 32, 1280), BF16),
    jax.ShapeDtypeStruct((10, 128, 1024), BF16),
)


def near_rows(g_own, a_own):
    return pl.pallas_call(
        near_kernel,
        out_shape=ROWS + (jax.ShapeDtypeStruct((16, 128), F32),),
        in_specs=[vmem(), vmem()],
        out_specs=(vmem(), vmem(), vmem()),
        compiler_params=pltpu.CompilerParams(vmem_limit_bytes=10 * 2**20),
        cost_estimate=pl.CostEstimate(flops=2**28, bytes_accessed=2**21, transcendentals=0),
        name="near_rows",
    )(g_own, a_own)


def filter_body(row, col, core, sums, g_nbr, a_nbr, abuf, gbuf, keep, send):
    act_rows(a_nbr, act_put(abuf, 4 - 4 * col))
    far_sums = cot_rows(g_nbr, 0, row, cot_put(gbuf, row, 1 - row))
    parts = []
    for slot in range(0, 10, 2):
        planes = range(max(slot - 2, 0), min(slot + 2, 8))
        moved = [abuf[plane, :, 128 * shift : 128 * shift + 1024] for plane in planes for shift in range(3)]
        parts.append(
            lax.dot_general(
                jnp.concatenate(moved, axis=0),
                gbuf[slot : slot + 2].reshape(256, 1024),
                NT,
                preferred_element_type=F32,
            )
        )
    whole = parts[1] + parts[2] + parts[3]
    wide = jnp.concatenate([whole[0:192] + parts[4], whole[192:384] + parts[0]], axis=0)
    acc = wide[0:288, 0:128] + wide[96:384, 128:256]
    side = jnp.concatenate([acc[216:288, 32 * m : 32 * m + 32] for m in range(3)], axis=0)
    table = jnp.concatenate([acc[0:216, 0:96], side], axis=1)
    first = jnp.where(row == 0, sums[...], far_sums)
    second = jnp.where(row == 0, far_sums, sums[...])
    column = jnp.sum(jnp.concatenate([first, second], axis=0), axis=1, keepdims=True)
    line = jnp.sum(jnp.where(iota((32, 128), 0) == iota((32, 128), 1), column, 0.0), axis=0, keepdims=True)
    bias = jnp.where(iota((8, 128), 0) == 0, line, 0.0)
    low = table[0:112]
    high = jnp.concatenate([table[112:216], bias], axis=0)
    keep[...] = jnp.where(core == 0, low, high)
    send[...] = jnp.where(core == 0, high, low)


def filter_kernel(a_in, g_in, sums, g_nbr, a_nbr, after, *outs):
    row, col, core = grid_place()
    for r in range(2):
        for c in range(2):
            pl.when((row == r) & (col == c))(
                functools.partial(filter_body, r, c, core, sums, g_nbr, a_nbr, *outs)
            )


def filter_partial(a_rows, g_rows, sums, g_nbr, a_nbr, after):
    half = jax.ShapeDtypeStruct((112, 128), F32)
    return pl.pallas_call(
        filter_kernel,
        out_shape=ROWS + (half, half),
        in_specs=[vmem()] * 5 + [anywhere()],
        out_specs=(vmem(),) * 4,
        input_output_aliases={0: 0, 1: 1},
        compiler_params=pltpu.CompilerParams(vmem_limit_bytes=12 * 2**20),
        cost_estimate=pl.CostEstimate(flops=2 * 10 * 288 * 96 * 1024, bytes_accessed=2**21, transcendentals=0),
        name="filter_partial",
    )(a_rows, g_rows, sums, g_nbr, a_nbr, after)[2:]


PASS = jax.ShapeDtypeStruct((16, 6, 8, 128), BF16)


def pass_kernel(near, g, after, out):
    row, col, _ = grid_place()
    first = 3 * (1 - col) + (7 * row if near else 0)
    for plane in range(6):
        out[:, plane] = g[:, first + plane]


def pass_on(g, after, near):
    return pl.pallas_call(
        functools.partial(pass_kernel, near),
        out_shape=PASS,
        in_specs=[vmem(), anywhere()],
        out_specs=vmem(),
        compiler_params=pltpu.CompilerParams(vmem_limit_bytes=4 * 2**20),
        cost_estimate=pl.CostEstimate(flops=2**30, bytes_accessed=2**23, transcendentals=0),
        name="pass_near" if near else "pass_on",
    )(g, after)


def finish_kernel(factor, mine, other, weight_out, bias_out):
    _, col, core = grid_place()
    lane = iota((224, 128), 1)
    tables = []
    for x in range(2):
        which = jnp.where(col == x, 0, 1)
        a, b = mine[which], other[which]
        low, high = jnp.where(core == 0, a, b), jnp.where(core == 0, b, a)
        tables.append(jnp.concatenate([low, high], axis=0) * factor)
    even = (lane & 16) == 0
    first = jnp.where(even, tables[0], pltpu.roll(tables[1], 16, 1))
    second = jnp.where(even, pltpu.roll(tables[0], 112, 1), tables[1])
    whole = []
    for dx in range(4):
        left = pltpu.roll(first, 128 - 32 * dx, 1) if dx else first
        right = pltpu.roll(second, (160 - 32 * dx) % 128, 1) if dx != 1 else second
        whole.append(jnp.where(lane < 32, left, right))
    for nine in range(9):
        for dx in range(3):
            k = 3 * nine + dx
            if nine < 6:
                weight_out[k] = whole[dx][32 * nine : 32 * nine + 32, 0:64]
            elif nine == 6:
                weight_out[k, 0:24] = whole[dx][192:216, 0:64]
                weight_out[k, 24:32] = whole[3][72 * dx : 72 * dx + 8, 0:64]
            else:
                at = 72 * dx + 32 * nine - 216
                weight_out[k] = whole[3][at : at + 32, 0:64]
    bias_out[...] = whole[0][216:217, 0:64]


def finish(mine, other, factor):
    return pl.pallas_call(
        functools.partial(finish_kernel, factor),
        out_shape=(jax.ShapeDtypeStruct((27, 32, 64), F32), jax.ShapeDtypeStruct((1, 64), F32)),
        in_specs=[vmem(), vmem()],
        out_specs=(vmem(), vmem()),
        compiler_params=pltpu.CompilerParams(vmem_limit_bytes=4 * 2**20),
        cost_estimate=pl.CostEstimate(flops=2**18, bytes_accessed=2**20, transcendentals=0),
        name="filter_finish",
    )(mine, other)


def spread_kernel(weight, after, out):
    place = lax.axis_index("slab")
    column = iota((64, 512), 1)
    block = column >> 7
    partner = jnp.where(block == 0, 0, jnp.where(block == 1, 2, jnp.where(block == 2, 1, 3)))
    slab = jnp.bitwise_xor(partner, place)
    repeat = one(iota((64, 512), 0) == 16 * slab + ((column & 127) >> 3))
    gap = iota((8, 128), 0) - (iota((8, 128), 1) & 7)
    masks = [gap == dy - 1 for dy in range(3)]
    for dz in range(3):
        for dx in range(3):
            wides = [
                jnp.dot(weight[9 * dz + 3 * dy + dx], repeat, preferred_element_type=F32) for dy in range(3)
            ]
            for m in range(4):
                cut = slice(128 * m, 128 * m + 128)
                band = jnp.zeros((32, 8, 128), F32)
                for dy in range(3):
                    w = jnp.broadcast_to(wides[dy][:, cut].reshape(32, 1, 128), (32, 8, 128))
                    band = jnp.where(jnp.broadcast_to(masks[dy][None], (32, 8, 128)), w, band)
                first = 256 * dz + 128 * (m % 2)
                out[m // 2, dx, :, first : first + 128] = band.reshape(256, 128).astype(BF16)


def spread_filters(weight, after):
    return pl.pallas_call(
        spread_kernel,
        out_shape=jax.ShapeDtypeStruct((2, 3, 256, 768), BF16),
        in_specs=[vmem(), anywhere()],
        out_specs=vmem(),
        compiler_params=pltpu.CompilerParams(vmem_limit_bytes=8 * 2**20),
        cost_estimate=pl.CostEstimate(flops=2 * 27 * 256 * 64 * 512, bytes_accessed=2**21, transcendentals=0),
        name="spread_filters",
    )(weight, after)


def stack_planes(offset, parts, stack):
    for index in range(-1, 5):
        at = offset + index
        inside = (at >= 0) & (at < 6)
        at = jnp.clip(at, 0, 5)
        for source, place, first in parts:
            chans = source.shape[0]
            value = source[:, place + at].reshape(8 * chans, 128)
            if index in (-1, 4):
                value = jnp.where(inside, value, jnp.zeros_like(value))
            for dz in range(3):
                z = index + dz - 1
                if 0 <= z < 4:
                    stack[256 * dz + first : 256 * dz + first + 8 * chans, 128 * z : 128 * z + 128] = value


def banded(spread, half, stack):
    lane = iota((256, 512), 1) & 127
    sums = [jnp.dot(spread[half, dx], stack[...], preferred_element_type=F32) for dx in range(3)]
    left = jnp.concatenate([pltpu.roll(sums[0][:, 128 * z : 128 * z + 128], 127, 1) for z in range(4)], axis=1)
    right = jnp.concatenate([pltpu.roll(sums[2][:, 128 * z : 128 * z + 128], 1, 1) for z in range(4)], axis=1)
    return sums[1] + jnp.where(lane == 127, 0.0, left) + jnp.where(lane == 0, 0.0, right)


def near_input_kernel(spread, g_own, g_nbr, out, stack):
    row, col, _ = grid_place()
    stack_planes(row + col, [(g_own, 7 * row + 3 * col, 0), (g_nbr, 3 * col, 128)], stack)
    out[...] = banded(spread, 0, stack)


def near_input(spread, g_own, g_nbr):
    return pl.pallas_call(
        near_input_kernel,
        out_shape=jax.ShapeDtypeStruct((256, 512), F32),
        in_specs=[vmem()] * 3,
        out_specs=vmem(),
        scratch_shapes=[pltpu.VMEM((768, 512), BF16)],
        compiler_params=pltpu.CompilerParams(vmem_limit_bytes=10 * 2**20),
        cost_estimate=pl.CostEstimate(flops=2**33, bytes_accessed=2**25, transcendentals=0),
        name="near_input",
    )(spread, g_own, g_nbr)


def far_input_kernel(spread, g_x, g_diag, near, out, mark, stack):
    row, col, _ = grid_place()
    stack_planes(row + col, [(g_x, 0, 0), (g_diag, 0, 128)], stack)
    total = (banded(spread, 1, stack) + near[...]).astype(BF16)
    for z in range(4):
        out[:, z] = total[:, 128 * z : 128 * z + 128].reshape(32, 8, 128)
    mark[...] = jnp.zeros((8, 128), F32)


def far_input(spread, g_x, g_diag, near):
    return pl.pallas_call(
        far_input_kernel,
        out_shape=(jax.ShapeDtypeStruct((32, 4, 8, 128), BF16), jax.ShapeDtypeStruct((8, 128), F32)),
        in_specs=[vmem()] * 4,
        out_specs=(vmem(), vmem()),
        scratch_shapes=[pltpu.VMEM((768, 512), BF16)],
        compiler_params=pltpu.CompilerParams(vmem_limit_bytes=10 * 2**20),
        cost_estimate=pl.CostEstimate(flops=9 * 256 * 256 * 512, bytes_accessed=2**22, transcendentals=0),
        name="far_input",
    )(spread, g_x, g_diag, near)


def swap(block, axis, bits):
    count = lax.axis_size(axis)
    return lax.ppermute(block, axis, [(i, i ^ bits) for i in range(count)])


def line_kernel(chip, one_off, two_off, both_off, after, out):
    out[...] = (chip[...] + one_off[...]) + (two_off[...] + both_off[...])


def line_sum(chip, one_off, two_off, both_off, after):
    return pl.pallas_call(
        line_kernel,
        out_shape=jax.ShapeDtypeStruct(chip.shape, F32),
        in_specs=[vmem()] * 4 + [anywhere()],
        out_specs=vmem(),
        compiler_params=pltpu.CompilerParams(vmem_limit_bytes=2**20),
        cost_estimate=pl.CostEstimate(flops=2**16, bytes_accessed=2**18, transcendentals=0),
        name="line_sum",
    )(chip, one_off, two_off, both_off, after)


def last_kernel(line, beside, across, diagonal, after, out):
    out[0] = line[...] + across[...]
    out[1] = beside[...] + diagonal[...]


def last_sum(line, beside, across, diagonal, after):
    return pl.pallas_call(
        last_kernel,
        out_shape=jax.ShapeDtypeStruct((2,) + line.shape, F32),
        in_specs=[vmem()] * 4 + [anywhere()],
        out_specs=vmem(),
        compiler_params=pltpu.CompilerParams(vmem_limit_bytes=2**20),
        cost_estimate=pl.CostEstimate(flops=2**16, bytes_accessed=2**18, transcendentals=0),
        name="last_sum",
    )(line, beside, across, diagonal, after)


def swap_at(block, slab_bits, sample_bits):
    count, samples = lax.axis_size(("slab", "sample")), lax.axis_size("sample")
    pairs = [(i, i ^ (samples * slab_bits + sample_bits)) for i in range(count)]
    return lax.ppermute(block, ("slab", "sample"), pairs)


def local_grid(activations, grad_out, weight):
    slab = lax.axis_index("slab")
    row = slab // 2
    act = activations[0]
    g_own = grad_out[0]

    a_nbr = swap(act, "slab", 1)
    g_nbr = swap(lax.dynamic_slice_in_dim(g_own, 7 * (1 - row), 9, axis=1), "slab", 2)
    a_rows, g_rows, sums = near_rows(g_own, act)
    spread = spread_filters(jnp.swapaxes(weight, 1, 2), sums)
    g_x = swap(pass_on(g_own, spread, True), "slab", 1)
    keep, send = filter_partial(a_rows, g_rows, sums, g_nbr, a_nbr, spread)
    chip = keep + swap(send, "sample", 1)
    g_diag = swap(pass_on(g_nbr, keep, False), "slab", 1)
    near = near_input(spread, g_own, g_nbr)
    line = line_sum(chip, swap_at(chip, 2, 0), swap_at(chip, 0, 2), swap_at(chip, 2, 2), near)
    grad_in, mark = far_input(spread, g_x, g_diag, near)
    mine = last_sum(line, swap_at(line, 1, 0), swap_at(line, 0, 4), swap_at(line, 1, 4), mark)
    other = swap(mine, "sample", 1)
    cells = 8 * 128 * 4 * lax.axis_size("slab") * lax.axis_size("sample")
    grad_weight, grad_bias = finish(mine, other, 1.0 / math.sqrt(cells))
    return grad_in[None], jnp.swapaxes(grad_weight, 1, 2), grad_bias.reshape(64)


def with_halo(block, sides, width):
    for axis, dim in sides:
        count = lax.axis_size(axis)
        forward = [(i, i + 1) for i in range(count - 1)]
        backward = [(target, source) for source, target in forward]
        low = lax.ppermute(
            lax.slice_in_dim(block, block.shape[dim] - width, None, axis=dim), axis, forward
        )
        high = lax.ppermute(lax.slice_in_dim(block, 0, width, axis=dim), axis, backward)
        block = jnp.concatenate([low, block, high], axis=dim)
    return block


def offsets_list():
    return [
        (shift_z, shift_y, shift_x)
        for shift_z in (-1, 0, 1)
        for shift_y in (-1, 0, 1)
        for shift_x in (-1, 0, 1)
    ]


def local_any(activations, grad_out, weight):
    samples, in_chan, planes, y_cells, x_cells = activations.shape
    slabs = lax.axis_size("slab")
    regrouped = lax.all_to_all(grad_out, "slab", split_axis=2, concat_axis=1, tiled=True)
    g_ext = with_halo(regrouped, (("slab", 2),), 1)
    widths = ((0, 0), (0, 0), (0, 0), (1, 1), (1, 1))
    padded_co = jnp.pad(g_ext, widths)
    grad_in = jnp.zeros((samples, in_chan, planes, y_cells, x_cells), F32)
    pieces = []
    for offset, (shift_z, shift_y, shift_x) in enumerate(offsets_list()):
        moved_co = padded_co[
            :,
            :,
            1 - shift_z : 1 - shift_z + planes,
            1 - shift_y : 1 - shift_y + y_cells,
            1 - shift_x : 1 - shift_x + x_cells,
        ]
        pieces.append(jnp.einsum("sozyx,sizyx->oi", moved_co, activations, preferred_element_type=F32))
        grad_in = grad_in + jnp.einsum("oi,sozyx->sizyx", weight[offset], moved_co, preferred_element_type=F32)
    wpart = jnp.stack(pieces)
    bpart = jnp.sum(regrouped.astype(F32), axis=(0, 2, 3, 4))
    wtotal, btotal = lax.psum((wpart, bpart), ("slab", "sample"))
    all_cells = samples * lax.axis_size("sample") * planes * slabs * y_cells * x_cells
    factor = 1.0 / math.sqrt(all_cells)
    return (grad_in.astype(BF16), wtotal * factor, btotal * factor)


def local(activations, grad_out, weight):
    grid = (
        lax.axis_size("slab") == 4
        and lax.axis_size("sample") == 8
        and activations.shape == (1, 32, 4, 8, 128)
        and grad_out.shape == (1, 16, 16, 8, 128)
    )
    return (local_grid if grid else local_any)(activations, grad_out, weight)


def solution(mesh):
    placed = (P("sample", None, "slab", None, None), P("sample", "slab", None, None, None), P())
    return jax.shard_map(
        local,
        mesh=mesh,
        in_specs=placed,
        out_specs=(P("sample", None, "slab", None, None), P(), P()),
        check_vma=False,
    )
```

```python
import functools
import math

import jax
import jax.numpy as jnp
from jax import lax
from jax.experimental import pallas as pl
from jax.experimental.pallas import tpu as pltpu
from jax.sharding import PartitionSpec as P

F32 = jnp.float32
BF16 = jnp.bfloat16
NT = (((1,), (1,)), ((), ()))


def iota(shape, dim):
    return lax.broadcasted_iota(jnp.int32, shape, dim)


def grid_place():
    slab = lax.axis_index("slab")
    return slab // 2, lax.rem(slab, 2), lax.rem(lax.axis_index("sample"), 2)


def vmem():
    return pl.BlockSpec(memory_space=pltpu.VMEM)


def anywhere():
    return pl.BlockSpec(memory_space=pl.ANY)


def one(mask):
    return mask.astype(F32).astype(BF16)


def act_rows(source, put):
    r, q = iota((256, 256), 0), iota((256, 256), 1)
    perm = one(((q & 7) == (r >> 5)) & ((q >> 3) == (r & 31)))
    both = jnp.concatenate([source[:, plane].reshape(256, 128) for plane in range(4)], axis=1)
    turned = jnp.dot(perm, both, preferred_element_type=F32).astype(BF16)
    for plane in range(4):
        for y in range(8):
            put(plane, y, turned[32 * y : 32 * y + 32, 128 * plane : 128 * plane + 128])


def cot_rows(source, first, row, put):
    r, q = iota((128, 128), 0), iota((128, 128), 1)
    perm = one(((q & 7) == (r >> 4)) & ((q >> 3) == (r & 15)))
    lane = iota((128, 128), 1)
    total = jnp.zeros((16, 128), F32)
    for plane in range(9):
        turned = jnp.dot(perm, source[:, first + plane].reshape(128, 128), preferred_element_type=F32)
        moved = (
            jnp.where(lane == 127, 0.0, pltpu.roll(turned, 127, 1)),
            turned,
            jnp.where(lane == 0, 0.0, pltpu.roll(turned, 1, 1)),
        )
        for shift in range(3):
            packed = moved[shift].astype(BF16)
            for y in range(8):
                put(plane, shift, y, packed[16 * y : 16 * y + 16])
        cells = turned[0:16]
        for y in range(1, 8):
            cells = cells + turned[16 * y : 16 * y + 16]
        if plane == 0:
            cells = jnp.where(row == 0, cells, 0.0)
        if plane == 8:
            cells = jnp.where(row == 0, 0.0, cells)
        total = total + cells
    return total


def act_put(abuf, first):
    def put(plane, y, piece):
        abuf[first + plane, :, 128 * y + 128 : 128 * y + 256] = piece

    return put


def cot_put(gbuf, row, whose):
    def put(plane, shift, y, piece):
        rows = pl.ds(pl.multiple_of(32 * shift + 16 * whose, 16), 16)
        gbuf[plane + 1 - row, rows, 128 * y : 128 * y + 128] = piece

    return put


def near_kernel(g_own, a_own, abuf, gbuf, sums):
    row, col, _ = grid_place()
    for plane in range(8):
        abuf[plane, :, 0:128] = jnp.zeros((32, 128), BF16)
        abuf[plane, :, 1152:1280] = jnp.zeros((32, 128), BF16)
    for slot in range(10):
        gbuf[slot, 96:128] = jnp.zeros((32, 1024), BF16)
    gbuf[9 * row] = jnp.zeros((128, 1024), BF16)
    act_rows(a_own, act_put(abuf, 4 * col))
    sums[...] = cot_rows(g_own, 7 * row, row, cot_put(gbuf, row, row))


ROWS = (
    jax.ShapeDtypeStruct((8, 32, 1280), BF16),
    jax.ShapeDtypeStruct((10, 128, 1024), BF16),
)


def near_rows(g_own, a_own):
    return pl.pallas_call(
        near_kernel,
        out_shape=ROWS + (jax.ShapeDtypeStruct((16, 128), F32),),
        in_specs=[vmem(), vmem()],
        out_specs=(vmem(), vmem(), vmem()),
        compiler_params=pltpu.CompilerParams(vmem_limit_bytes=10 * 2**20),
        cost_estimate=pl.CostEstimate(flops=2**28, bytes_accessed=2**21, transcendentals=0),
        name="near_rows",
    )(g_own, a_own)


def filter_body(row, col, core, sums, g_nbr, a_nbr, abuf, gbuf, keep, send):
    act_rows(a_nbr, act_put(abuf, 4 - 4 * col))
    far_sums = cot_rows(g_nbr, 0, row, cot_put(gbuf, row, 1 - row))
    parts = []
    for slot in range(0, 10, 2):
        planes = range(max(slot - 2, 0), min(slot + 2, 8))
        moved = [abuf[plane, :, 128 * shift : 128 * shift + 1024] for plane in planes for shift in range(3)]
        parts.append(
            lax.dot_general(
                jnp.concatenate(moved, axis=0),
                gbuf[slot : slot + 2].reshape(256, 1024),
                NT,
                preferred_element_type=F32,
            )
        )
    whole = parts[1] + parts[2] + parts[3]
    wide = jnp.concatenate([whole[0:192] + parts[4], whole[192:384] + parts[0]], axis=0)
    acc = wide[0:288, 0:128] + wide[96:384, 128:256]
    side = jnp.concatenate([acc[216:288, 32 * m : 32 * m + 32] for m in range(3)], axis=0)
    table = jnp.concatenate([acc[0:216, 0:96], side], axis=1)
    first = jnp.where(row == 0, sums[...], far_sums)
    second = jnp.where(row == 0, far_sums, sums[...])
    column = jnp.sum(jnp.concatenate([first, second], axis=0), axis=1, keepdims=True)
    line = jnp.sum(jnp.where(iota((32, 128), 0) == iota((32, 128), 1), column, 0.0), axis=0, keepdims=True)
    bias = jnp.where(iota((8, 128), 0) == 0, line, 0.0)
    low = table[0:112]
    high = jnp.concatenate([table[112:216], bias], axis=0)
    keep[...] = jnp.where(core == 0, low, high)
    send[...] = jnp.where(core == 0, high, low)


def filter_kernel(a_in, g_in, sums, g_nbr, a_nbr, after, *outs):
    row, col, core = grid_place()
    for r in range(2):
        for c in range(2):
            pl.when((row == r) & (col == c))(
                functools.partial(filter_body, r, c, core, sums, g_nbr, a_nbr, *outs)
            )


def filter_partial(a_rows, g_rows, sums, g_nbr, a_nbr, after):
    half = jax.ShapeDtypeStruct((112, 128), F32)
    return pl.pallas_call(
        filter_kernel,
        out_shape=ROWS + (half, half),
        in_specs=[vmem()] * 5 + [anywhere()],
        out_specs=(vmem(),) * 4,
        input_output_aliases={0: 0, 1: 1},
        compiler_params=pltpu.CompilerParams(vmem_limit_bytes=12 * 2**20),
        cost_estimate=pl.CostEstimate(flops=2 * 10 * 288 * 96 * 1024, bytes_accessed=2**21, transcendentals=0),
        name="filter_partial",
    )(a_rows, g_rows, sums, g_nbr, a_nbr, after)[2:]


def pass_kernel(g_own, g_nbr, after, out):
    row, col, _ = grid_place()
    for plane in range(6):
        out[0:16, plane] = g_own[:, 7 * row + 3 * (1 - col) + plane]
        out[16:32, plane] = g_nbr[:, 3 * (1 - col) + plane]


def pass_on(g_own, g_nbr, after):
    return pl.pallas_call(
        pass_kernel,
        out_shape=jax.ShapeDtypeStruct((32, 6, 8, 128), BF16),
        in_specs=[vmem(), vmem(), anywhere()],
        out_specs=vmem(),
        compiler_params=pltpu.CompilerParams(vmem_limit_bytes=4 * 2**20),
        cost_estimate=pl.CostEstimate(flops=2**30, bytes_accessed=2**23, transcendentals=0),
        name="pass_on",
    )(g_own, g_nbr, after)


def arranged(factor, col, halves):
    lane = iota((112, 128), 1)
    tables = [halves[jnp.where(col == x, 0, 1)] * factor for x in range(2)]
    even = (lane & 16) == 0
    first = jnp.where(even, tables[0], pltpu.roll(tables[1], 16, 1))
    second = jnp.where(even, pltpu.roll(tables[0], 112, 1), tables[1])
    whole = []
    for dx in range(4):
        left = pltpu.roll(first, 128 - 32 * dx, 1) if dx else first
        right = pltpu.roll(second, (160 - 32 * dx) % 128, 1) if dx != 1 else second
        whole.append(jnp.where(lane < 32, left, right))
    return whole


def prepare_kernel(factor, mine, out):
    _, col, _ = grid_place()
    for dx, value in enumerate(arranged(factor, col, mine)):
        out[dx] = value


def prepare(mine, factor):
    return pl.pallas_call(
        functools.partial(prepare_kernel, factor),
        out_shape=jax.ShapeDtypeStruct((4, 112, 128), F32),
        in_specs=[vmem()],
        out_specs=vmem(),
        compiler_params=pltpu.CompilerParams(vmem_limit_bytes=2 * 2**20),
        cost_estimate=pl.CostEstimate(flops=2**18, bytes_accessed=2**19, transcendentals=0),
        name="prepare",
    )(mine)


def finish_body(core, ready, other, weight_out, bias_out):
    whole = []
    for dx in range(4):
        halves = (ready[dx], other[dx]) if core == 0 else (other[dx], ready[dx])
        whole.append(jnp.concatenate(halves, axis=0))
    for nine in range(9):
        for dx in range(3):
            k = 3 * nine + dx
            if nine < 6:
                weight_out[k] = whole[dx][32 * nine : 32 * nine + 32, 0:64]
            elif nine == 6:
                weight_out[k, 0:24] = whole[dx][192:216, 0:64]
                weight_out[k, 24:32] = whole[3][72 * dx : 72 * dx + 8, 0:64]
            else:
                at = 72 * dx + 32 * nine - 216
                weight_out[k] = whole[3][at : at + 32, 0:64]
    bias_out[...] = whole[0][216:217, 0:64]


def finish_kernel(factor, ready, other, weight_out, bias_out):
    _, col, core = grid_place()
    for c in range(2):

        @pl.when(core == c)
        def _(c=c):
            finish_body(c, ready, arranged(factor, col, other), weight_out, bias_out)


def finish(ready, other, factor):
    return pl.pallas_call(
        functools.partial(finish_kernel, factor),
        out_shape=(jax.ShapeDtypeStruct((27, 32, 64), F32), jax.ShapeDtypeStruct((1, 64), F32)),
        in_specs=[vmem(), vmem()],
        out_specs=(vmem(), vmem()),
        compiler_params=pltpu.CompilerParams(vmem_limit_bytes=4 * 2**20),
        cost_estimate=pl.CostEstimate(flops=2**18, bytes_accessed=2**20, transcendentals=0),
        name="filter_finish",
    )(ready, other)


def spread_kernel(weight, after, out):
    place = lax.axis_index("slab")
    column = iota((64, 512), 1)
    block = column >> 7
    partner = jnp.where(block == 0, 0, jnp.where(block == 1, 2, jnp.where(block == 2, 1, 3)))
    slab = jnp.bitwise_xor(partner, place)
    repeat = one(iota((64, 512), 0) == 16 * slab + ((column & 127) >> 3))
    gap = iota((8, 128), 0) - (iota((8, 128), 1) & 7)
    masks = [gap == dy - 1 for dy in range(3)]
    for dz in range(3):
        for dx in range(3):
            wides = [
                jnp.dot(weight[9 * dz + 3 * dy + dx], repeat, preferred_element_type=F32) for dy in range(3)
            ]
            for m in range(4):
                cut = slice(128 * m, 128 * m + 128)
                band = jnp.zeros((32, 8, 128), F32)
                for dy in range(3):
                    w = jnp.broadcast_to(wides[dy][:, cut].reshape(32, 1, 128), (32, 8, 128))
                    band = jnp.where(jnp.broadcast_to(masks[dy][None], (32, 8, 128)), w, band)
                first = 256 * dz + 128 * (m % 2)
                out[m // 2, dx, :, first : first + 128] = band.reshape(256, 128).astype(BF16)


def spread_filters(weight, after):
    return pl.pallas_call(
        spread_kernel,
        out_shape=jax.ShapeDtypeStruct((2, 3, 256, 768), BF16),
        in_specs=[vmem(), anywhere()],
        out_specs=vmem(),
        compiler_params=pltpu.CompilerParams(vmem_limit_bytes=8 * 2**20),
        cost_estimate=pl.CostEstimate(flops=2 * 27 * 256 * 64 * 512, bytes_accessed=2**21, transcendentals=0),
        name="spread_filters",
    )(weight, after)


def stack_planes(offset, parts, stack):
    for index in range(-1, 5):
        at = offset + index
        inside = (at >= 0) & (at < 6)
        at = jnp.clip(at, 0, 5)
        for source, place, first in parts:
            chans = source.shape[0]
            value = source[:, place + at].reshape(8 * chans, 128)
            if index in (-1, 4):
                value = jnp.where(inside, value, jnp.zeros_like(value))
            for dz in range(3):
                z = index + dz - 1
                if 0 <= z < 4:
                    stack[256 * dz + first : 256 * dz + first + 8 * chans, 128 * z : 128 * z + 128] = value


def banded(spread, half, stack):
    lane = iota((256, 512), 1) & 127
    sums = [jnp.dot(spread[half, dx], stack[...], preferred_element_type=F32) for dx in range(3)]
    left = jnp.concatenate([pltpu.roll(sums[0][:, 128 * z : 128 * z + 128], 127, 1) for z in range(4)], axis=1)
    right = jnp.concatenate([pltpu.roll(sums[2][:, 128 * z : 128 * z + 128], 1, 1) for z in range(4)], axis=1)
    return sums[1] + jnp.where(lane == 127, 0.0, left) + jnp.where(lane == 0, 0.0, right)


def near_input_kernel(spread, g_own, g_nbr, out, stack):
    row, col, _ = grid_place()
    stack_planes(row + col, [(g_own, 7 * row + 3 * col, 0), (g_nbr, 3 * col, 128)], stack)
    out[...] = banded(spread, 0, stack)


def near_input(spread, g_own, g_nbr):
    return pl.pallas_call(
        near_input_kernel,
        out_shape=jax.ShapeDtypeStruct((256, 512), F32),
        in_specs=[vmem()] * 3,
        out_specs=vmem(),
        scratch_shapes=[pltpu.VMEM((768, 512), BF16)],
        compiler_params=pltpu.CompilerParams(vmem_limit_bytes=10 * 2**20),
        cost_estimate=pl.CostEstimate(flops=2**33, bytes_accessed=2**25, transcendentals=0),
        name="near_input",
    )(spread, g_own, g_nbr)


def far_input_kernel(spread, g_far, near, out, mark, stack):
    row, col, _ = grid_place()
    stack_planes(row + col, [(g_far, 0, 0)], stack)
    total = (banded(spread, 1, stack) + near[...]).astype(BF16)
    for z in range(4):
        out[:, z] = total[:, 128 * z : 128 * z + 128].reshape(32, 8, 128)
    mark[...] = jnp.zeros((8, 128), F32)


def far_input(spread, g_far, near):
    return pl.pallas_call(
        far_input_kernel,
        out_shape=(jax.ShapeDtypeStruct((32, 4, 8, 128), BF16), jax.ShapeDtypeStruct((8, 128), F32)),
        in_specs=[vmem()] * 3,
        out_specs=(vmem(), vmem()),
        scratch_shapes=[pltpu.VMEM((768, 512), BF16)],
        compiler_params=pltpu.CompilerParams(vmem_limit_bytes=10 * 2**20),
        cost_estimate=pl.CostEstimate(flops=9 * 256 * 256 * 512, bytes_accessed=2**22, transcendentals=0),
        name="far_input",
    )(spread, g_far, near)


def swap(block, axis, bits):
    count = lax.axis_size(axis)
    return lax.ppermute(block, axis, [(i, i ^ bits) for i in range(count)])


def line_kernel(chip, one_off, two_off, both_off, after, out):
    out[...] = (chip[...] + one_off[...]) + (two_off[...] + both_off[...])


def line_sum(chip, one_off, two_off, both_off, after):
    return pl.pallas_call(
        line_kernel,
        out_shape=jax.ShapeDtypeStruct(chip.shape, F32),
        in_specs=[vmem()] * 4 + [anywhere()],
        out_specs=vmem(),
        compiler_params=pltpu.CompilerParams(vmem_limit_bytes=2**20),
        cost_estimate=pl.CostEstimate(flops=2**16, bytes_accessed=2**18, transcendentals=0),
        name="line_sum",
    )(chip, one_off, two_off, both_off, after)


def last_kernel(line, beside, across, diagonal, after, out):
    out[0] = line[...] + across[...]
    out[1] = beside[...] + diagonal[...]


def last_sum(line, beside, across, diagonal, after):
    return pl.pallas_call(
        last_kernel,
        out_shape=jax.ShapeDtypeStruct((2,) + line.shape, F32),
        in_specs=[vmem()] * 4 + [anywhere()],
        out_specs=vmem(),
        compiler_params=pltpu.CompilerParams(vmem_limit_bytes=2**20),
        cost_estimate=pl.CostEstimate(flops=2**16, bytes_accessed=2**18, transcendentals=0),
        name="last_sum",
    )(line, beside, across, diagonal, after)


def swap_at(block, slab_bits, sample_bits):
    count, samples = lax.axis_size(("slab", "sample")), lax.axis_size("sample")
    pairs = [(i, i ^ (samples * slab_bits + sample_bits)) for i in range(count)]
    return lax.ppermute(block, ("slab", "sample"), pairs)


def local_grid(activations, grad_out, weight):
    slab = lax.axis_index("slab")
    row = slab // 2
    act = activations[0]
    g_own = grad_out[0]

    a_nbr = swap(act, "slab", 1)
    g_nbr = swap(lax.dynamic_slice_in_dim(g_own, 7 * (1 - row), 9, axis=1), "slab", 2)
    a_rows, g_rows, sums = near_rows(g_own, act)
    spread = spread_filters(jnp.swapaxes(weight, 1, 2), sums)
    keep, send = filter_partial(a_rows, g_rows, sums, g_nbr, a_nbr, spread)
    chip = keep + swap(send, "sample", 1)
    g_far = swap(pass_on(g_own, g_nbr, keep), "slab", 1)
    near = near_input(spread, g_own, g_nbr)
    line = line_sum(chip, swap_at(chip, 2, 0), swap_at(chip, 0, 2), swap_at(chip, 2, 2), near)
    grad_in, mark = far_input(spread, g_far, near)
    mine = last_sum(line, swap_at(line, 1, 0), swap_at(line, 0, 4), swap_at(line, 1, 4), mark)
    other = swap(mine, "sample", 1)
    cells = 8 * 128 * 4 * lax.axis_size("slab") * lax.axis_size("sample")
    factor = 1.0 / math.sqrt(cells)
    grad_weight, grad_bias = finish(prepare(mine, factor), other, factor)
    return grad_in[None], jnp.swapaxes(grad_weight, 1, 2), grad_bias.reshape(64)


def with_halo(block, sides, width):
    for axis, dim in sides:
        count = lax.axis_size(axis)
        forward = [(i, i + 1) for i in range(count - 1)]
        backward = [(target, source) for source, target in forward]
        low = lax.ppermute(
            lax.slice_in_dim(block, block.shape[dim] - width, None, axis=dim), axis, forward
        )
        high = lax.ppermute(lax.slice_in_dim(block, 0, width, axis=dim), axis, backward)
        block = jnp.concatenate([low, block, high], axis=dim)
    return block


def offsets_list():
    return [
        (shift_z, shift_y, shift_x)
        for shift_z in (-1, 0, 1)
        for shift_y in (-1, 0, 1)
        for shift_x in (-1, 0, 1)
    ]


def local_any(activations, grad_out, weight):
    samples, in_chan, planes, y_cells, x_cells = activations.shape
    slabs = lax.axis_size("slab")
    regrouped = lax.all_to_all(grad_out, "slab", split_axis=2, concat_axis=1, tiled=True)
    g_ext = with_halo(regrouped, (("slab", 2),), 1)
    widths = ((0, 0), (0, 0), (0, 0), (1, 1), (1, 1))
    padded_co = jnp.pad(g_ext, widths)
    grad_in = jnp.zeros((samples, in_chan, planes, y_cells, x_cells), F32)
    pieces = []
    for offset, (shift_z, shift_y, shift_x) in enumerate(offsets_list()):
        moved_co = padded_co[
            :,
            :,
            1 - shift_z : 1 - shift_z + planes,
            1 - shift_y : 1 - shift_y + y_cells,
            1 - shift_x : 1 - shift_x + x_cells,
        ]
        pieces.append(jnp.einsum("sozyx,sizyx->oi", moved_co, activations, preferred_element_type=F32))
        grad_in = grad_in + jnp.einsum("oi,sozyx->sizyx", weight[offset], moved_co, preferred_element_type=F32)
    wpart = jnp.stack(pieces)
    bpart = jnp.sum(regrouped.astype(F32), axis=(0, 2, 3, 4))
    wtotal, btotal = lax.psum((wpart, bpart), ("slab", "sample"))
    all_cells = samples * lax.axis_size("sample") * planes * slabs * y_cells * x_cells
    factor = 1.0 / math.sqrt(all_cells)
    return (grad_in.astype(BF16), wtotal * factor, btotal * factor)


def local(activations, grad_out, weight):
    grid = (
        lax.axis_size("slab") == 4
        and lax.axis_size("sample") == 8
        and activations.shape == (1, 32, 4, 8, 128)
        and grad_out.shape == (1, 16, 16, 8, 128)
    )
    return (local_grid if grid else local_any)(activations, grad_out, weight)


def solution(mesh):
    placed = (P("sample", None, "slab", None, None), P("sample", "slab", None, None, None), P())
    return jax.shard_map(
        local,
        mesh=mesh,
        in_specs=placed,
        out_specs=(P("sample", None, "slab", None, None), P(), P()),
        check_vma=False,
    )
```

```python
import functools
import math

import jax
import jax.numpy as jnp
from jax import lax
from jax.experimental import pallas as pl
from jax.experimental.pallas import tpu as pltpu
from jax.sharding import PartitionSpec as P

F32 = jnp.float32
BF16 = jnp.bfloat16
NT = (((1,), (1,)), ((), ()))


def iota(shape, dim):
    return lax.broadcasted_iota(jnp.int32, shape, dim)


def grid_place():
    slab = lax.axis_index("slab")
    return slab // 2, lax.rem(slab, 2), lax.rem(lax.axis_index("sample"), 2)


def vmem():
    return pl.BlockSpec(memory_space=pltpu.VMEM)


def anywhere():
    return pl.BlockSpec(memory_space=pl.ANY)


def one(mask):
    return mask.astype(F32).astype(BF16)


def act_rows(source, put):
    r, q = iota((256, 256), 0), iota((256, 256), 1)
    perm = one(((q & 7) == (r >> 5)) & ((q >> 3) == (r & 31)))
    both = jnp.concatenate([source[:, plane].reshape(256, 128) for plane in range(4)], axis=1)
    turned = jnp.dot(perm, both, preferred_element_type=F32).astype(BF16)
    for plane in range(4):
        for y in range(8):
            put(plane, y, turned[32 * y : 32 * y + 32, 128 * plane : 128 * plane + 128])


def cot_rows(source, first, row, put):
    r, q = iota((128, 128), 0), iota((128, 128), 1)
    perm = one(((q & 7) == (r >> 4)) & ((q >> 3) == (r & 15)))
    lane = iota((128, 128), 1)
    total = jnp.zeros((16, 128), F32)
    for plane in range(9):
        turned = jnp.dot(perm, source[:, first + plane].reshape(128, 128), preferred_element_type=F32)
        moved = (
            jnp.where(lane == 127, 0.0, pltpu.roll(turned, 127, 1)),
            turned,
            jnp.where(lane == 0, 0.0, pltpu.roll(turned, 1, 1)),
        )
        for shift in range(3):
            packed = moved[shift].astype(BF16)
            for y in range(8):
                put(plane, shift, y, packed[16 * y : 16 * y + 16])
        cells = turned[0:16]
        for y in range(1, 8):
            cells = cells + turned[16 * y : 16 * y + 16]
        if plane == 0:
            cells = jnp.where(row == 0, cells, 0.0)
        if plane == 8:
            cells = jnp.where(row == 0, 0.0, cells)
        total = total + cells
    return total


def act_put(abuf, first):
    def put(plane, y, piece):
        abuf[first + plane, :, 128 * y + 128 : 128 * y + 256] = piece

    return put


def cot_put(gbuf, row, whose):
    def put(plane, shift, y, piece):
        rows = pl.ds(pl.multiple_of(32 * shift + 16 * whose, 16), 16)
        gbuf[plane + 1 - row, rows, 128 * y : 128 * y + 128] = piece

    return put


def near_kernel(g_own, a_own, abuf, gbuf, sums):
    row, col, _ = grid_place()
    for plane in range(8):
        abuf[plane, :, 0:128] = jnp.zeros((32, 128), BF16)
        abuf[plane, :, 1152:1280] = jnp.zeros((32, 128), BF16)
    for slot in range(10):
        gbuf[slot, 96:128] = jnp.zeros((32, 1024), BF16)
    gbuf[9 * row] = jnp.zeros((128, 1024), BF16)
    act_rows(a_own, act_put(abuf, 4 * col))
    sums[...] = cot_rows(g_own, 7 * row, row, cot_put(gbuf, row, row))


ROWS = (
    jax.ShapeDtypeStruct((8, 32, 1280), BF16),
    jax.ShapeDtypeStruct((10, 128, 1024), BF16),
)


def near_rows(g_own, a_own):
    return pl.pallas_call(
        near_kernel,
        out_shape=ROWS + (jax.ShapeDtypeStruct((16, 128), F32),),
        in_specs=[vmem(), vmem()],
        out_specs=(vmem(), vmem(), vmem()),
        compiler_params=pltpu.CompilerParams(vmem_limit_bytes=10 * 2**20),
        cost_estimate=pl.CostEstimate(flops=2**28, bytes_accessed=2**21, transcendentals=0),
        name="near_rows",
    )(g_own, a_own)


def filter_body(row, col, core, sums, g_nbr, a_nbr, abuf, gbuf, keep, send):
    act_rows(a_nbr, act_put(abuf, 4 - 4 * col))
    far_sums = cot_rows(g_nbr, 0, row, cot_put(gbuf, row, 1 - row))
    parts = []
    for slot in range(0, 10, 2):
        planes = range(max(slot - 2, 0), min(slot + 2, 8))
        moved = [abuf[plane, :, 128 * shift : 128 * shift + 1024] for plane in planes for shift in range(3)]
        parts.append(
            lax.dot_general(
                jnp.concatenate(moved, axis=0),
                gbuf[slot : slot + 2].reshape(256, 1024),
                NT,
                preferred_element_type=F32,
            )
        )
    whole = parts[1] + parts[2] + parts[3]
    wide = jnp.concatenate([whole[0:192] + parts[4], whole[192:384] + parts[0]], axis=0)
    acc = wide[0:288, 0:128] + wide[96:384, 128:256]
    side = jnp.concatenate([acc[216:288, 32 * m : 32 * m + 32] for m in range(3)], axis=0)
    table = jnp.concatenate([acc[0:216, 0:96], side], axis=1)
    first = jnp.where(row == 0, sums[...], far_sums)
    second = jnp.where(row == 0, far_sums, sums[...])
    column = jnp.sum(jnp.concatenate([first, second], axis=0), axis=1, keepdims=True)
    line = jnp.sum(jnp.where(iota((32, 128), 0) == iota((32, 128), 1), column, 0.0), axis=0, keepdims=True)
    bias = jnp.where(iota((8, 128), 0) == 0, line, 0.0)
    low = table[0:112]
    high = jnp.concatenate([table[112:216], bias], axis=0)
    keep[...] = jnp.where(core == 0, low, high)
    send[...] = jnp.where(core == 0, high, low)


def filter_kernel(a_in, g_in, sums, g_nbr, a_nbr, after, *outs):
    row, col, core = grid_place()
    for r in range(2):
        pl.when(row == r)(functools.partial(filter_body, r, col, core, sums, g_nbr, a_nbr, *outs))


def filter_partial(a_rows, g_rows, sums, g_nbr, a_nbr, after):
    half = jax.ShapeDtypeStruct((112, 128), F32)
    return pl.pallas_call(
        filter_kernel,
        out_shape=ROWS + (half, half),
        in_specs=[vmem()] * 5 + [anywhere()],
        out_specs=(vmem(),) * 4,
        input_output_aliases={0: 0, 1: 1},
        compiler_params=pltpu.CompilerParams(vmem_limit_bytes=12 * 2**20),
        cost_estimate=pl.CostEstimate(flops=2 * 10 * 288 * 96 * 1024, bytes_accessed=2**21, transcendentals=0),
        name="filter_partial",
    )(a_rows, g_rows, sums, g_nbr, a_nbr, after)[2:]


def pass_kernel(g_own, g_nbr, after, out):
    row, col, _ = grid_place()
    for plane in range(6):
        out[0:16, plane] = g_own[:, 7 * row + 3 * (1 - col) + plane]
        out[16:32, plane] = g_nbr[:, 3 * (1 - col) + plane]


def pass_on(g_own, g_nbr, after):
    return pl.pallas_call(
        pass_kernel,
        out_shape=jax.ShapeDtypeStruct((32, 6, 8, 128), BF16),
        in_specs=[vmem(), vmem(), anywhere()],
        out_specs=vmem(),
        compiler_params=pltpu.CompilerParams(vmem_limit_bytes=4 * 2**20),
        cost_estimate=pl.CostEstimate(flops=2**30, bytes_accessed=2**23, transcendentals=0),
        name="pass_on",
    )(g_own, g_nbr, after)


def arranged(factor, col, halves):
    lane = iota((112, 128), 1)
    tables = [halves[jnp.where(col == x, 0, 1)] * factor for x in range(2)]
    even = (lane & 16) == 0
    first = jnp.where(even, tables[0], pltpu.roll(tables[1], 16, 1))
    second = jnp.where(even, pltpu.roll(tables[0], 112, 1), tables[1])
    whole = []
    for dx in range(4):
        left = pltpu.roll(first, 128 - 32 * dx, 1) if dx else first
        right = pltpu.roll(second, (160 - 32 * dx) % 128, 1) if dx != 1 else second
        whole.append(jnp.where(lane < 32, left, right))
    return whole


def prepare_kernel(factor, mine, out):
    _, col, _ = grid_place()
    for dx, value in enumerate(arranged(factor, col, mine)):
        out[dx] = value


def prepare(mine, factor):
    return pl.pallas_call(
        functools.partial(prepare_kernel, factor),
        out_shape=jax.ShapeDtypeStruct((4, 112, 128), F32),
        in_specs=[vmem()],
        out_specs=vmem(),
        compiler_params=pltpu.CompilerParams(vmem_limit_bytes=2 * 2**20),
        cost_estimate=pl.CostEstimate(flops=2**18, bytes_accessed=2**19, transcendentals=0),
        name="prepare",
    )(mine)


def finish_body(core, ready, other, weight_out, bias_out):
    whole = []
    for dx in range(4):
        halves = (ready[dx], other[dx]) if core == 0 else (other[dx], ready[dx])
        whole.append(jnp.concatenate(halves, axis=0))
    for nine in range(9):
        for dx in range(3):
            k = 3 * nine + dx
            if nine < 6:
                weight_out[k] = whole[dx][32 * nine : 32 * nine + 32, 0:64]
            elif nine == 6:
                weight_out[k, 0:24] = whole[dx][192:216, 0:64]
                weight_out[k, 24:32] = whole[3][72 * dx : 72 * dx + 8, 0:64]
            else:
                at = 72 * dx + 32 * nine - 216
                weight_out[k] = whole[3][at : at + 32, 0:64]
    bias_out[...] = whole[0][216:217, 0:64]


def finish_kernel(factor, ready, other, weight_out, bias_out):
    _, col, core = grid_place()
    for c in range(2):

        @pl.when(core == c)
        def _(c=c):
            finish_body(c, ready, arranged(factor, col, other), weight_out, bias_out)


def finish(ready, other, factor):
    return pl.pallas_call(
        functools.partial(finish_kernel, factor),
        out_shape=(jax.ShapeDtypeStruct((27, 32, 64), F32), jax.ShapeDtypeStruct((1, 64), F32)),
        in_specs=[vmem(), vmem()],
        out_specs=(vmem(), vmem()),
        compiler_params=pltpu.CompilerParams(vmem_limit_bytes=4 * 2**20),
        cost_estimate=pl.CostEstimate(flops=2**18, bytes_accessed=2**20, transcendentals=0),
        name="filter_finish",
    )(ready, other)


def spread_kernel(weight, after, out):
    place = lax.axis_index("slab")
    column = iota((64, 512), 1)
    block = column >> 7
    partner = jnp.where(block == 0, 0, jnp.where(block == 1, 2, jnp.where(block == 2, 1, 3)))
    slab = jnp.bitwise_xor(partner, place)
    repeat = one(iota((64, 512), 0) == 16 * slab + ((column & 127) >> 3))
    gap = iota((8, 128), 0) - (iota((8, 128), 1) & 7)
    masks = [gap == dy - 1 for dy in range(3)]
    for dz in range(3):
        for dx in range(3):
            wides = [
                jnp.dot(weight[9 * dz + 3 * dy + dx], repeat, preferred_element_type=F32) for dy in range(3)
            ]
            for m in range(4):
                cut = slice(128 * m, 128 * m + 128)
                band = jnp.zeros((32, 8, 128), F32)
                for dy in range(3):
                    w = jnp.broadcast_to(wides[dy][:, cut].reshape(32, 1, 128), (32, 8, 128))
                    band = jnp.where(jnp.broadcast_to(masks[dy][None], (32, 8, 128)), w, band)
                first = 256 * dz + 128 * (m % 2)
                out[m // 2, dx, :, first : first + 128] = band.reshape(256, 128).astype(BF16)


def spread_filters(weight, after):
    return pl.pallas_call(
        spread_kernel,
        out_shape=jax.ShapeDtypeStruct((2, 3, 256, 768), BF16),
        in_specs=[vmem(), anywhere()],
        out_specs=vmem(),
        compiler_params=pltpu.CompilerParams(vmem_limit_bytes=8 * 2**20),
        cost_estimate=pl.CostEstimate(flops=2 * 27 * 256 * 64 * 512, bytes_accessed=2**21, transcendentals=0),
        name="spread_filters",
    )(weight, after)


def stack_planes(offset, parts, stack):
    for index in range(-1, 5):
        at = offset + index
        inside = (at >= 0) & (at < 6)
        at = jnp.clip(at, 0, 5)
        for source, place, first in parts:
            chans = source.shape[0]
            value = source[:, place + at].reshape(8 * chans, 128)
            if index in (-1, 4):
                value = jnp.where(inside, value, jnp.zeros_like(value))
            for dz in range(3):
                z = index + dz - 1
                if 0 <= z < 4:
                    stack[256 * dz + first : 256 * dz + first + 8 * chans, 128 * z : 128 * z + 128] = value


def banded(spread, half, stack):
    lane = iota((256, 512), 1) & 127
    sums = [jnp.dot(spread[half, dx], stack[...], preferred_element_type=F32) for dx in range(3)]
    left = jnp.concatenate([pltpu.roll(sums[0][:, 128 * z : 128 * z + 128], 127, 1) for z in range(4)], axis=1)
    right = jnp.concatenate([pltpu.roll(sums[2][:, 128 * z : 128 * z + 128], 1, 1) for z in range(4)], axis=1)
    return sums[1] + jnp.where(lane == 127, 0.0, left) + jnp.where(lane == 0, 0.0, right)


def near_input_kernel(spread, g_own, g_nbr, out, stack):
    row, col, _ = grid_place()
    stack_planes(row + col, [(g_own, 7 * row + 3 * col, 0), (g_nbr, 3 * col, 128)], stack)
    out[...] = banded(spread, 0, stack)


def near_input(spread, g_own, g_nbr):
    return pl.pallas_call(
        near_input_kernel,
        out_shape=jax.ShapeDtypeStruct((256, 512), F32),
        in_specs=[vmem()] * 3,
        out_specs=vmem(),
        scratch_shapes=[pltpu.VMEM((768, 512), BF16)],
        compiler_params=pltpu.CompilerParams(vmem_limit_bytes=10 * 2**20),
        cost_estimate=pl.CostEstimate(flops=2**33, bytes_accessed=2**25, transcendentals=0),
        name="near_input",
    )(spread, g_own, g_nbr)


def far_input_kernel(spread, g_far, near, out, mark, stack):
    row, col, _ = grid_place()
    stack_planes(row + col, [(g_far, 0, 0)], stack)
    total = (banded(spread, 1, stack) + near[...]).astype(BF16)
    for z in range(4):
        out[:, z] = total[:, 128 * z : 128 * z + 128].reshape(32, 8, 128)
    mark[...] = jnp.zeros((8, 128), F32)


def far_input(spread, g_far, near):
    return pl.pallas_call(
        far_input_kernel,
        out_shape=(jax.ShapeDtypeStruct((32, 4, 8, 128), BF16), jax.ShapeDtypeStruct((8, 128), F32)),
        in_specs=[vmem()] * 3,
        out_specs=(vmem(), vmem()),
        scratch_shapes=[pltpu.VMEM((768, 512), BF16)],
        compiler_params=pltpu.CompilerParams(vmem_limit_bytes=10 * 2**20),
        cost_estimate=pl.CostEstimate(flops=9 * 256 * 256 * 512, bytes_accessed=2**22, transcendentals=0),
        name="far_input",
    )(spread, g_far, near)


def swap(block, axis, bits):
    count = lax.axis_size(axis)
    return lax.ppermute(block, axis, [(i, i ^ bits) for i in range(count)])


def line_kernel(chip, one_off, two_off, both_off, after, out):
    out[...] = (chip[...] + one_off[...]) + (two_off[...] + both_off[...])


def line_sum(chip, one_off, two_off, both_off, after):
    return pl.pallas_call(
        line_kernel,
        out_shape=jax.ShapeDtypeStruct(chip.shape, F32),
        in_specs=[vmem()] * 4 + [anywhere()],
        out_specs=vmem(),
        compiler_params=pltpu.CompilerParams(vmem_limit_bytes=2**20),
        cost_estimate=pl.CostEstimate(flops=2**16, bytes_accessed=2**18, transcendentals=0),
        name="line_sum",
    )(chip, one_off, two_off, both_off, after)


def last_kernel(line, beside, across, diagonal, after, out):
    out[0] = line[...] + across[...]
    out[1] = beside[...] + diagonal[...]


def last_sum(line, beside, across, diagonal, after):
    return pl.pallas_call(
        last_kernel,
        out_shape=jax.ShapeDtypeStruct((2,) + line.shape, F32),
        in_specs=[vmem()] * 4 + [anywhere()],
        out_specs=vmem(),
        compiler_params=pltpu.CompilerParams(vmem_limit_bytes=2**20),
        cost_estimate=pl.CostEstimate(flops=2**16, bytes_accessed=2**18, transcendentals=0),
        name="last_sum",
    )(line, beside, across, diagonal, after)


def swap_at(block, slab_bits, sample_bits):
    count, samples = lax.axis_size(("slab", "sample")), lax.axis_size("sample")
    pairs = [(i, i ^ (samples * slab_bits + sample_bits)) for i in range(count)]
    return lax.ppermute(block, ("slab", "sample"), pairs)


def local_grid(activations, grad_out, weight):
    slab = lax.axis_index("slab")
    row = slab // 2
    act = activations[0]
    g_own = grad_out[0]

    a_nbr = swap(act, "slab", 1)
    g_nbr = swap(lax.dynamic_slice_in_dim(g_own, 7 * (1 - row), 9, axis=1), "slab", 2)
    a_rows, g_rows, sums = near_rows(g_own, act)
    spread = spread_filters(jnp.swapaxes(weight, 1, 2), sums)
    keep, send = filter_partial(a_rows, g_rows, sums, g_nbr, a_nbr, spread)
    chip = keep + swap(send, "sample", 1)
    g_far = swap(pass_on(g_own, g_nbr, keep), "slab", 1)
    near = near_input(spread, g_own, g_nbr)
    line = line_sum(chip, swap_at(chip, 2, 0), swap_at(chip, 0, 2), swap_at(chip, 2, 2), near)
    grad_in, mark = far_input(spread, g_far, near)
    mine = last_sum(line, swap_at(line, 1, 0), swap_at(line, 0, 4), swap_at(line, 1, 4), mark)
    other = swap(mine, "sample", 1)
    cells = 8 * 128 * 4 * lax.axis_size("slab") * lax.axis_size("sample")
    factor = 1.0 / math.sqrt(cells)
    grad_weight, grad_bias = finish(prepare(mine, factor), other, factor)
    return grad_in[None], jnp.swapaxes(grad_weight, 1, 2), grad_bias.reshape(64)


def with_halo(block, sides, width):
    for axis, dim in sides:
        count = lax.axis_size(axis)
        forward = [(i, i + 1) for i in range(count - 1)]
        backward = [(target, source) for source, target in forward]
        low = lax.ppermute(
            lax.slice_in_dim(block, block.shape[dim] - width, None, axis=dim), axis, forward
        )
        high = lax.ppermute(lax.slice_in_dim(block, 0, width, axis=dim), axis, backward)
        block = jnp.concatenate([low, block, high], axis=dim)
    return block


def offsets_list():
    return [
        (shift_z, shift_y, shift_x)
        for shift_z in (-1, 0, 1)
        for shift_y in (-1, 0, 1)
        for shift_x in (-1, 0, 1)
    ]


def local_any(activations, grad_out, weight):
    samples, in_chan, planes, y_cells, x_cells = activations.shape
    slabs = lax.axis_size("slab")
    regrouped = lax.all_to_all(grad_out, "slab", split_axis=2, concat_axis=1, tiled=True)
    g_ext = with_halo(regrouped, (("slab", 2),), 1)
    widths = ((0, 0), (0, 0), (0, 0), (1, 1), (1, 1))
    padded_co = jnp.pad(g_ext, widths)
    grad_in = jnp.zeros((samples, in_chan, planes, y_cells, x_cells), F32)
    pieces = []
    for offset, (shift_z, shift_y, shift_x) in enumerate(offsets_list()):
        moved_co = padded_co[
            :,
            :,
            1 - shift_z : 1 - shift_z + planes,
            1 - shift_y : 1 - shift_y + y_cells,
            1 - shift_x : 1 - shift_x + x_cells,
        ]
        pieces.append(jnp.einsum("sozyx,sizyx->oi", moved_co, activations, preferred_element_type=F32))
        grad_in = grad_in + jnp.einsum("oi,sozyx->sizyx", weight[offset], moved_co, preferred_element_type=F32)
    wpart = jnp.stack(pieces)
    bpart = jnp.sum(regrouped.astype(F32), axis=(0, 2, 3, 4))
    wtotal, btotal = lax.psum((wpart, bpart), ("slab", "sample"))
    all_cells = samples * lax.axis_size("sample") * planes * slabs * y_cells * x_cells
    factor = 1.0 / math.sqrt(all_cells)
    return (grad_in.astype(BF16), wtotal * factor, btotal * factor)


def local(activations, grad_out, weight):
    grid = (
        lax.axis_size("slab") == 4
        and lax.axis_size("sample") == 8
        and activations.shape == (1, 32, 4, 8, 128)
        and grad_out.shape == (1, 16, 16, 8, 128)
    )
    return (local_grid if grid else local_any)(activations, grad_out, weight)


def solution(mesh):
    placed = (P("sample", None, "slab", None, None), P("sample", "slab", None, None, None), P())
    return jax.shard_map(
        local,
        mesh=mesh,
        in_specs=placed,
        out_specs=(P("sample", None, "slab", None, None), P(), P()),
        check_vma=False,
    )
```
